256 devices in a mesh: dp: 8 (over y, x_hi), seq: 32 (over z, x_lo, core).
Axes of the slice: x: 4 (x_hi: 2, x_lo: 2; x = x_hi * 2 + x_lo), y: 4, z: 8, core: 2. Of those that a mesh axis runs over, the one named last changes fastest.
Arguments:
- hidden: bfloat16 [1024, 4096], P('dp')
- gain: float32 [4096], replicated, may hold values from 0.5 to 1.5
- head_weight: bfloat16 [84224, 4096], P('seq', 'dp')
- targets: int32 [1024], P('dp'), may hold values from 0 to 84223
- loss_mask: int32 [1024], P('dp'), may hold values from 0 to 1, as said below
Outputs:
- loss: float32 [], replicated
- grad_hidden: bfloat16 [1024, 4096], P('dp')
- grad_gain: float32 [4096], replicated
- grad_head: float32 [84224, 4096], P('seq', 'dp')
The draws below stay inside these ranges and needn't reach their ends.
Inputs may be any that keep to these rules, and one draw needn't show every extreme that they name: `loss_mask`: position 0 is valid; the share of valid positions rises from about a quarter at the first position to about three quarters at the last.
All inputs are finite; a program needn't handle non-finite values.
Results may differ from the reference program's by a relative error of at most 0.0049.
Values may be sent and summed in bfloat16 or wider, within the bound.
A program may use at most 64 MiB of HBM per device.

```python
import math
import jax
import jax.numpy as jnp
import numpy as np
from jax import lax

D = 4096
TOK_DEV = 128
TOKENS = 1024
VOCAB = 84224


def draw_hidden(key, part):
    key = jax.random.fold_in(key, 11)
    values = jax.random.normal(key, (TOKENS, D), jnp.float32)
    return values.astype(jnp.bfloat16)


def draw_head_weight(key, part):
    key = jax.random.fold_in(key, 23)
    values = jax.random.normal(key, (VOCAB, D), jnp.float32) / D ** 0.5
    return values.astype(jnp.bfloat16)


def draw_loss_mask(key, part):
    key = jax.random.fold_in(key, 37)
    place = jnp.arange(TOKENS, dtype=jnp.int32)
    drawn = jax.random.randint(key, (TOKENS,), 0, 4 * TOKENS, dtype=jnp.int32)
    valid = (drawn < TOKENS + 2 * place).astype(jnp.int32)
    return valid.at[0].set(1)


def set_ends(values, own_key, smallest, largest):
    dims = values.shape
    index_at = [jax.random.randint(jax.random.fold_in(own_key, axis), (), 0, dims[axis]) for axis in range(len(dims))]
    values = values.at[tuple(index_at)].set(smallest)
    longest = dims.index(max(dims))
    index_at[longest] = (index_at[longest] + 1) % dims[longest]
    return values.at[tuple(index_at)].set(largest)


def ranked_wide(stream_key, shape, amount, lean):
    portions = [min(1 << octave, amount + 1 - (1 << octave)) * (1 << 20) // math.isqrt((1 << octave) ** lean) + 1 for octave in range((amount + 1).bit_length()) if 1 << octave <= amount]
    scale = 1 + sum(portions) // (1 << 30)
    table = np.cumsum(np.array([max(1, weight // scale) for weight in portions]))
    ticket = jax.random.randint(jax.random.fold_in(stream_key, 1), shape, 0, int(table[len(portions) - 1]))
    start = jnp.left_shift(1, jnp.searchsorted(jnp.asarray(table, jnp.int32), ticket, side="right").astype(jnp.int32))
    grade = start - 1 + jax.random.randint(jax.random.fold_in(stream_key, 4), shape, 0, 1 << 30) % jnp.minimum(start, amount + 1 - start)
    return jax.random.permutation(jax.random.fold_in(stream_key, 2), amount)[grade].astype(jnp.int32)


def setup_inputs(seed: int = 0) -> dict:
    keys = jax.random.split(jax.random.key(seed), 6)
    hidden = draw_hidden(jax.random.fold_in(keys[5], 71), 0)
    gain = jnp.clip(jax.random.uniform(keys[1], (D,), jnp.float32, 0.5, 1.5), 0.5, 1.5)
    head_weight = draw_head_weight(jax.random.fold_in(keys[5], 71), 0)
    targets = set_ends(ranked_wide(keys[3], (TOKENS,), VOCAB, 2), jax.random.fold_in(keys[3], 3), 0, VOCAB - 1).astype(jnp.int32)
    loss_mask = draw_loss_mask(jax.random.fold_in(keys[5], 71), 0)
    return dict(hidden=hidden, gain=gain, head_weight=head_weight, targets=targets, loss_mask=loss_mask)


EPS = 1e-05

def block_terms(row_block, pick_block, valid_block, gain, weight, num_valid):
    floats = row_block.astype(jnp.float32)
    inv_rms = lax.rsqrt(lax.optimization_barrier(jnp.mean(floats * floats, axis=-1, keepdims=True)) + EPS)
    unit_rows = floats * inv_rms
    normed = (unit_rows * gain).astype(jnp.bfloat16)
    logits = lax.dot_general(normed, weight, (((1,), (1,)), ((), ())), preferred_element_type=jnp.float32)
    row_top = lax.optimization_barrier(jnp.max(logits, axis=1, keepdims=True))
    shifted = jnp.exp(logits - row_top)
    row_total = lax.optimization_barrier(jnp.sum(shifted, axis=1, keepdims=True))
    log_total = row_top + jnp.log(row_total)
    probs = shifted / row_total
    column = jnp.arange(logits.shape[1], dtype=jnp.int32)
    one_hot = (column[None, :] == pick_block[:, None]).astype(jnp.float32)
    picked = lax.optimization_barrier(jnp.sum(one_hot * logits, axis=1))
    row_loss = log_total[:, 0] - picked
    mask_float = valid_block.astype(jnp.float32)
    dlogits = ((probs - one_hot) * (mask_float / num_valid)[:, None]).astype(jnp.bfloat16)
    dnormed = jnp.dot(dlogits, weight, preferred_element_type=jnp.float32)
    head_part = lax.dot_general(dlogits, normed, (((0,), (0,)), ((), ())), preferred_element_type=jnp.float32)
    gain_part = lax.optimization_barrier(jnp.sum(dnormed * unit_rows, axis=0))
    grad_unit = dnormed * gain
    grad_rows = inv_rms * (grad_unit - unit_rows * lax.optimization_barrier(jnp.mean(grad_unit * unit_rows, axis=-1, keepdims=True)))
    return (jnp.sum(mask_float * row_loss), head_part, gain_part, grad_rows.astype(jnp.bfloat16))

def reference(hidden, gain, head_weight, targets, loss_mask):
    num_valid = jnp.sum(loss_mask.astype(jnp.float32))
    blocks = TOKENS // TOK_DEV
    rows_all = hidden.reshape(blocks, TOK_DEV, D)
    picks_all = targets.reshape(blocks, TOK_DEV)
    valid_all = loss_mask.reshape(blocks, TOK_DEV)

    def advance(carry, item):
        loss_sum, head_sum, gain_sum = carry
        row_block, pick_block, valid_block = item
        part_loss, head_part, gain_part, grad_rows = block_terms(row_block, pick_block, valid_block, gain, head_weight, num_valid)
        return ((loss_sum + part_loss, head_sum + head_part, gain_sum + gain_part), grad_rows)
    initial = (jnp.zeros((), jnp.float32), jnp.zeros((VOCAB, D), jnp.float32), jnp.zeros((D,), jnp.float32))
    (loss_sum, grad_head, grad_gain), grad_blocks = lax.scan(advance, initial, (rows_all, picks_all, valid_all))
    loss_value = loss_sum / num_valid
    return (loss_value, grad_blocks.reshape(TOKENS, D), grad_gain, grad_head)
```

```python
import jax
import jax.numpy as jnp
from jax import lax
from jax.experimental import pallas as pl
from jax.experimental.pallas import tpu as pltpu
from jax.sharding import PartitionSpec as P

EPS = 1e-05
MESH = pl.DeviceIdType.MESH
F32 = jnp.float32
BF16 = jnp.bfloat16
NT = (((1,), (1,)), ((), ()))

D = 4096
W = 512
B = 128
V = 2632
CAP = 640
CH = 7
R = 384
LOW = -1e30

H0, M0, HC0, S10, S20, SX0 = 0, 8, 16, 24, 32, 40
T10, T20, T30, GX0, G20, G10 = 48, 56, 64, 72, 80, 88
DC0, DX0, DZ0, DP0, AZ0, BZ0, AX0, BX0, AC0, BC0 = 96, 97, 104, 112, 120, 128, 136, 137, 138, 139
NSEM = 144


def kernel(hid, gain, wgt, tgt, msk, gh, ghid, gg, scal,
           H, META, WT, S, HC, HCT, C, GCOL, ROWS, L, R1, A1, R2, A2, R3, F, STAT, ST1, ST2, ST3,
           DL, DN, RC, T1, B1, RX, T2, B2, RZ, MB, RB, GT, GG, GH, ss, rs, ls):
    dp = lax.axis_index("dp")
    seq = lax.axis_index("seq")
    y, xh = dp // 2, dp % 2
    z, xl, co = seq // 4, (seq // 2) % 2, seq % 2
    p1, p2 = (y // 2 + y) % 2, y // 2
    ya, yb = y + 1 - 2 * (y % 2), 3 - y
    xpeer = y * 2 + 1 - xh

    def seq_of(zz, xx, cc):
        return zz * 4 + xx * 2 + cc

    def rcopy(src, dst, sem, dev):
        return pltpu.make_async_remote_copy(
            src_ref=src, dst_ref=dst, send_sem=ss.at[sem], recv_sem=rs.at[sem],
            device_id=dev, device_id_type=MESH)

    dp_peers = [lax.rem(dp + k, 8) for k in range(1, 8)]
    dp_from = [lax.rem(dp + 8 - k, 8) for k in range(1, 8)]
    z_peers = [lax.rem(z + k, 8) for k in range(1, 8)]
    z_from = [lax.rem(z + 8 - k, 8) for k in range(1, 8)]
    g_me = xl * 2 + co
    g_peers = [lax.rem(g_me + k, 4) for k in range(1, 4)]
    g_from = [lax.rem(g_me + 4 - k, 4) for k in range(1, 4)]
    core_dev = (dp, seq_of(z, xl, 1 - co))
    xlo_dev = (dp, seq_of(z, 1 - xl, co))

    barrier = pltpu.get_barrier_semaphore()
    for j in dp_peers:
        pl.semaphore_signal(barrier, inc=1, device_id=(j, seq), device_id_type=MESH)
    for g in g_peers:
        pl.semaphore_signal(barrier, inc=1, device_id=(dp, z * 4 + g), device_id_type=MESH)
    for zz in z_peers:
        pl.semaphore_signal(barrier, inc=1, device_id=(dp, seq_of(zz, xl, co)), device_id_type=MESH)
    pl.semaphore_wait(barrier, 17)

    half = pl.ds(pl.multiple_of(co * 64, 64), 64)
    ohalf = pl.ds(pl.multiple_of((1 - co) * 64, 64), 64)
    hsend = []
    for k in range(1, 8):
        j = dp_peers[k - 1]
        c = rcopy(hid.at[half, pl.ds(pl.multiple_of(j * W, W), W)], H.at[dp, half, :], H0 + k, (j, seq))
        c.start()
        hsend.append(c)
    H[dp] = hid[:, pl.ds(pl.multiple_of(dp * W, W), W)]
    total = jnp.zeros((B, 1), F32)
    for j in range(8):
        x = hid[:, j * W:(j + 1) * W].astype(F32)
        total = total + jnp.sum(x * x, axis=1, keepdims=True)
    rinv = lax.rsqrt(total * (1.0 / D) + EPS)
    rinv_t = jnp.transpose(jnp.broadcast_to(rinv, (B, B)))
    META[dp] = jnp.concatenate(
        [rinv_t[0:1, :], msk[...].astype(F32), tgt[...].astype(F32), jnp.zeros((5, B), F32)], axis=0)
    msend = []
    for k in range(1, 8):
        c = rcopy(META.at[dp], META.at[dp], M0 + k, (dp_peers[k - 1], seq))
        c.start()
        msend.append(c)

    @pl.loop(0, CH)
    def _(c):
        rows = pl.ds(pl.multiple_of(c * R, R), R)
        WT[c] = jnp.transpose(wgt[rows, :])
    gain_row = gain[pl.ds(dp, 1), :]
    GCOL[...] = jnp.transpose(jnp.broadcast_to(gain_row, (B, W)))

    hc = []
    for k in range(1, 8):
        j = dp_from[k - 1]
        rcopy(H.at[j, half, :], H.at[j, half, :], H0 + k, (dp, seq)).wait_recv()
        c = rcopy(H.at[j, half, :], H.at[j, half, :], HC0 + k, core_dev)
        c.start()
        hc.append(c)
    for k in range(1, 8):
        j = dp_from[k - 1]
        rcopy(META.at[j], META.at[j], M0 + k, (dp, seq)).wait_recv()

    metas = [META[j] for j in range(8)]
    m8 = jnp.concatenate([m[1:2, :] for m in metas] + [jnp.zeros((8, B), F32)], axis=0)
    tri = (lax.broadcasted_iota(jnp.int32, (B, B), 0) <= lax.broadcasted_iota(jnp.int32, (B, B), 1)).astype(F32)
    cum = jnp.dot(m8.astype(BF16), tri.astype(BF16), preferred_element_type=F32)
    base = jnp.zeros((1, 1), F32)
    slot = lax.broadcasted_iota(jnp.int32, (CAP, B), 0)
    for j in range(8):
        rank = jnp.where(metas[j][1:2, :] > 0.5, cum[j:j + 1, :] + base - 1.0, -1.0).astype(jnp.int32)
        S[:, j * B:(j + 1) * B] = (slot == rank).astype(F32).astype(BF16)
        base = base + jnp.sum(metas[j][1:2, :], axis=1, keepdims=True)
    count = base
    r_all = jnp.concatenate([m[0:1, :] for m in metas], axis=1)
    v_all = jnp.concatenate([m[1:2, :] for m in metas], axis=1)
    t_all = jnp.concatenate([m[2:3, :] for m in metas], axis=1)
    hi = r_all.astype(BF16).astype(F32)
    mid = (r_all - hi).astype(BF16).astype(F32)
    lo = (r_all - hi) - mid
    ta = jnp.floor(t_all * (1.0 / 4096))
    tb = jnp.floor((t_all - ta * 4096) * (1.0 / 64))
    tc = t_all - ta * 4096 - tb * 64
    mr = jnp.concatenate([hi, mid, lo, v_all, ta, tb, tc, jnp.zeros((9, 8 * B), F32)], axis=0).astype(BF16)
    crow = lax.dot_general(mr, S[...], NT, preferred_element_type=F32)
    mr2 = jnp.concatenate([mr, jnp.zeros((B - 16, 8 * B), BF16)], axis=0)
    ccol = lax.dot_general(S[...], mr2, NT, preferred_element_type=F32)
    rinv_row = crow[0:1, :] + crow[1:2, :] + crow[2:3, :]
    valid_row = crow[3:4, :]
    tgt_f = crow[4:5, :] * 4096.0 + crow[5:6, :] * 64.0 + crow[6:7, :]
    tgt_f = jnp.where(valid_row > 0.5, tgt_f, -1.0)
    rinv_col = ccol[:, 0:1] + ccol[:, 1:2] + ccol[:, 2:3]
    share = valid_row / count
    ROWS[...] = jnp.concatenate([rinv_row, share, tgt_f, valid_row, jnp.zeros((4, CAP), F32)], axis=0)

    for k in range(1, 8):
        j = dp_from[k - 1]
        rcopy(H.at[j, ohalf, :], H.at[j, ohalf, :], HC0 + k, core_dev).wait_recv()
    hcomp = jnp.dot(S[...], H[...].reshape(8 * B, W), preferred_element_type=F32)
    C[...] = ((hcomp * rinv_col) * gain_row).astype(BF16)
    HCT[...] = jnp.transpose(hcomp)
    STAT[...] = jnp.concatenate([jnp.full((1, CAP), LOW, F32), jnp.zeros((7, CAP), F32)], axis=0)

    def order(c):
        odd = c % 2
        first = p1 * (1 - odd) + p2 * odd
        second = p2 * (1 - odd) + p1 * odd
        dev1 = (ya * (1 - odd) + yb * odd) * 2 + xh
        dev2 = (yb * (1 - odd) + ya * odd) * 2 + xh
        return first, second, (dev1, seq), (dev2, seq)

    def rows_at(start, size):
        return pl.ds(pl.multiple_of(start, 16), size)

    xdev = (xpeer, seq)

    def s1(c):
        f, g, dev1, dev2 = order(c)
        return rcopy(L.at[c, rows_at((1 - f) * 192, 192), :], R1.at[c], S10 + c, dev1)

    def s2(c):
        f, g, dev1, dev2 = order(c)
        return rcopy(A1.at[c, rows_at((1 - g) * 96, 96), :], R2.at[c], S20 + c, dev2)

    def sx(c):
        return rcopy(A2.at[c, rows_at((1 - xh) * 48, 48), :], R3.at[c], SX0 + c, xdev)

    def piece(c):
        f, g, dev1, dev2 = order(c)
        return f * 192 + g * 96 + xh * 48

    def marks(c):
        local = c * R + piece(c) + lax.broadcasted_iota(jnp.int32, (48, CAP), 0)
        inside = local < V
        hit = jnp.logical_and(inside, (local + seq * V) == ROWS[2:3, :].astype(jnp.int32))
        return inside, hit

    LAG1, LAG2, LAG3 = 2, 4, 6

    @pl.loop(0, CH + LAG3)
    def _(k):
        @pl.when(k < CH)
        def _():
            rows = pl.ds(pl.multiple_of(k * R, R), R)
            L[k] = lax.dot_general(wgt[rows, :], C[...], NT, preferred_element_type=F32).astype(BF16)
            s1(k).start()

        @pl.when(jnp.logical_and(k >= LAG1, k < CH + LAG1))
        def _():
            c = k - LAG1
            f, g, dev1, dev2 = order(c)
            s1(c).wait_recv()
            A1[c] = (L[c, rows_at(f * 192, 192), :].astype(F32) + R1[c].astype(F32)).astype(BF16)
            s2(c).start()

        @pl.when(jnp.logical_and(k >= LAG2, k < CH + LAG2))
        def _():
            c = k - LAG2
            f, g, dev1, dev2 = order(c)
            s2(c).wait_recv()
            A2[c] = (A1[c, rows_at(g * 96, 96), :].astype(F32) + R2[c].astype(F32)).astype(BF16)
            sx(c).start()

        @pl.when(k >= LAG3)
        def _():
            c = k - LAG3
            sx(c).wait_recv()
            logits = A2[c, rows_at(xh * 48, 48), :].astype(F32) + R3[c].astype(F32)
            inside, hit = marks(c)
            logits = jnp.where(inside, logits, LOW)
            F[c] = logits
            old = STAT[0:1, :]
            top = jnp.maximum(old, jnp.max(logits, axis=0, keepdims=True))
            ex = jnp.where(inside, jnp.exp(logits - top), 0.0)
            scale = jnp.exp(old - top)
            STAT[1:2, :] = STAT[1:2, :] * scale + jnp.sum(ex, axis=0, keepdims=True)
            STAT[2:3, :] = STAT[2:3, :] * scale + jnp.sum(ex * logits, axis=0, keepdims=True)
            STAT[3:4, :] = STAT[3:4, :] + jnp.sum(jnp.where(hit, logits, 0.0), axis=0, keepdims=True)
            STAT[0:1, :] = top

    def merge(slots, n):
        parts = [slots[i] for i in range(n)]
        top = parts[0][0:1, :]
        for q in parts[1:]:
            top = jnp.maximum(top, q[0:1, :])
        ssum = jnp.zeros((1, CAP), F32)
        esum = jnp.zeros((1, CAP), F32)
        tsum = jnp.zeros((1, CAP), F32)
        for q in parts:
            w = jnp.exp(q[0:1, :] - top)
            ssum = ssum + q[1:2, :] * w
            esum = esum + q[2:3, :] * w
            tsum = tsum + q[3:4, :]
        return top, ssum, esum, tsum

    def packed(vals):
        return jnp.concatenate(list(vals) + [jnp.zeros((4, CAP), F32)], axis=0)

    sends = []

    def spread(slots, mine, devs, froms, sem):
        for k, dev in enumerate(devs, 1):
            c = rcopy(slots.at[mine], slots.at[mine], sem + k, dev)
            c.start()
            sends.append(c)
        for k, src in enumerate(froms, 1):
            rcopy(slots.at[src], slots.at[src], sem + k, (dp, seq)).wait_recv()

    ST1[g_me] = STAT[...]
    spread(ST1, g_me, [(dp, z * 4 + g) for g in g_peers], g_from, T10)
    ST2[z] = packed(merge(ST1, 4))
    spread(ST2, z, [(dp, seq_of(zz, xl, co)) for zz in z_peers], z_from, T20)
    ST3[dp] = packed(merge(ST2, 8))
    spread(ST3, dp, [(j, seq) for j in dp_peers], dp_from, T30)
    top, ssum, esum, tsum = merge(ST3, 8)
    share = ROWS[1:2, :]
    valid_row = ROWS[3:4, :]
    log_total = jnp.log(ssum) + top
    loss = jnp.sum(jnp.where(valid_row > 0.5, log_total - tsum, 0.0), axis=1, keepdims=True) / count
    peak = jnp.where(valid_row > 0.5, (1.0 + jnp.abs(top)) / ssum, 0.0)
    worst = jnp.max(peak, axis=1, keepdims=True)
    wide = jnp.where(count > CAP + 0.5, 1.0, 0.0)
    other = jnp.where(worst > 0.25, 1.0, 0.0)
    scal[...] = jnp.concatenate([
        jnp.broadcast_to(loss, (1, B)), jnp.broadcast_to(jnp.maximum(wide, other), (1, B)),
        jnp.zeros((6, B), F32)], axis=0)
    ROWS[4:5, :] = top
    ROWS[5:6, :] = share / ssum
    ROWS[6:7, :] = (esum / ssum - tsum) * share * (1.0 / D)
    DN[...] = jnp.zeros_like(DN)

    def gx(c):
        me = rows_at(piece(c), 48)
        return rcopy(DL.at[c, me, :], DL.at[c, me, :], GX0 + c, xdev)

    def gx_in(c):
        f, g, dev1, dev2 = order(c)
        at = rows_at(f * 192 + g * 96 + (1 - xh) * 48, 48)
        return rcopy(DL.at[c, at, :], DL.at[c, at, :], GX0 + c, xdev)

    def g2(c):
        f, g, dev1, dev2 = order(c)
        me = rows_at(f * 192 + g * 96, 96)
        return rcopy(DL.at[c, me, :], DL.at[c, me, :], G20 + c, dev2)

    def g2_in(c):
        f, g, dev1, dev2 = order(c)
        at = rows_at(f * 192 + (1 - g) * 96, 96)
        return rcopy(DL.at[c, at, :], DL.at[c, at, :], G20 + c, dev2)

    def g1(c):
        f, g, dev1, dev2 = order(c)
        me = rows_at(f * 192, 192)
        return rcopy(DL.at[c, me, :], DL.at[c, me, :], G10 + c, dev1)

    def g1_in(c):
        f, g, dev1, dev2 = order(c)
        at = rows_at((1 - f) * 192, 192)
        return rcopy(DL.at[c, at, :], DL.at[c, at, :], G10 + c, dev1)

    @pl.loop(0, CH)
    def _(c):
        inside, hit = marks(c)
        probs = jnp.exp(F[c] - ROWS[4:5, :]) * ROWS[5:6, :]
        DL[c, rows_at(piece(c), 48), :] = (probs - jnp.where(hit, ROWS[1:2, :], 0.0)).astype(BF16)
        gx(c).start()

    K2, K3 = 2, 4

    @pl.loop(0, CH + K3)
    def _(k):
        @pl.when(k < CH)
        def _():
            gx_in(k).wait_recv()
            g2(k).start()

        @pl.when(jnp.logical_and(k >= K2, k < CH + K2))
        def _():
            c = k - K2
            g2_in(c).wait_recv()
            g1(c).start()

        @pl.when(k >= K3)
        def _():
            c = k - K3
            g1_in(c).wait_recv()
            DN[...] += jnp.dot(WT[c], DL[c], preferred_element_type=F32)

    def grad_chunk(c):
        GH[c] = lax.dot_general(DL[c], C[...], (((1,), (0,)), ((), ())), preferred_element_type=F32)

    def head_copy(c):
        n = R if c < CH - 1 else V - R * (CH - 1)
        return pltpu.make_async_copy(GH.at[c, pl.ds(0, n), :], gh.at[pl.ds(c * R, n), :], ls.at[c])

    dc = rcopy(DN.at[rows_at((1 - co) * 256, 256), :], RC, DC0, core_dev)
    dc.start()
    grad_chunk(0)
    head_copy(0).start()
    dc.wait_recv()
    T1[...] = DN[rows_at(co * 256, 256), :] + RC[...]
    B1[...] = T1[rows_at((1 - xl) * 128, 128), :].astype(BF16)
    dx = rcopy(B1, RX, DX0, xlo_dev)
    dx.start()
    for c in (1, 2, 3):
        grad_chunk(c)
        head_copy(c).start()
    dx.wait_recv()
    T2[...] = T1[rows_at(xl * 128, 128), :] + RX[...].astype(F32)
    for i in range(8):
        B2[i] = T2[i * 16:(i + 1) * 16, :].astype(BF16)
    dz = []
    for k in range(1, 8):
        c = rcopy(B2.at[z_peers[k - 1]], RZ.at[z], DZ0 + k, (dp, seq_of(z_peers[k - 1], xl, co)))
        c.start()
        dz.append(c)
    for c in (4, 5, 6):
        grad_chunk(c)
        head_copy(c).start()
    for k in range(1, 8):
        rcopy(RZ.at[z_from[k - 1]], RZ.at[z_from[k - 1]], DZ0 + k, (dp, seq)).wait_recv()
    dn = T2[rows_at(z * 16, 16), :]
    for k in range(1, 8):
        dn = dn + RZ[z_from[k - 1]].astype(F32)

    off = co * 256 + xl * 128 + z * 16
    rinv_row = ROWS[0:1, :]
    xn = HCT[rows_at(off, 16), :] * rinv_row
    gc = GCOL[rows_at(off, 16), 0:1]
    grow = (rinv_row * (dn * gc - xn * ROWS[6:7, :])).astype(BF16)
    ggc = jnp.sum(dn * xn, axis=1, keepdims=True)
    wide_rows = jnp.dot(grow, S[...], preferred_element_type=F32).astype(BF16)
    ghi = ggc.astype(BF16).astype(F32)
    gmid = (ggc - ghi).astype(BF16).astype(F32)
    glo = (ggc - ghi) - gmid
    lane = lax.broadcasted_iota(jnp.int32, (16, B), 1)
    gparts = jnp.where(lane == 0, ghi, jnp.where(lane == 1, gmid, jnp.where(lane == 2, glo, 0.0))).astype(BF16)
    for j in range(8):
        MB[j, 0:16, :] = wide_rows[:, j * B:(j + 1) * B]
        MB[j, 16:32, :] = gparts
    dpc = []
    for k in range(1, 8):
        c = rcopy(MB.at[dp_peers[k - 1]], RB.at[dp], DP0 + k, (dp_peers[k - 1], seq))
        c.start()
        dpc.append(c)
    RB[dp] = MB[dp]
    for k in range(1, 8):
        rcopy(RB.at[dp_from[k - 1]], RB.at[dp_from[k - 1]], DP0 + k, (dp, seq)).wait_recv()

    mine = rows_at(off, 16)
    for j in range(8):
        GT[j, mine, :] = RB[j, 0:16, :]
    gsum = jnp.transpose(RB[:, 16:32, :].reshape(B, B).astype(F32))
    grow1 = gsum[0:1, :] + gsum[1:2, :] + gsum[2:3, :]
    gidx = co * 16 + xl * 8 + z
    GG[gidx] = jnp.broadcast_to(grow1, (8, B))
    for k in range(1, 8):
        dev = (dp, seq_of(z_peers[k - 1], xl, co))
        c = rcopy(GT.at[:, mine, :], GT.at[:, mine, :], AZ0 + k, dev)
        c.start()
        sends.append(c)
        c = rcopy(GG.at[gidx], GG.at[gidx], BZ0 + k, dev)
        c.start()
        sends.append(c)
    for k in range(1, 8):
        zf = z_from[k - 1]
        at = rows_at(co * 256 + xl * 128 + zf * 16, 16)
        rcopy(GT.at[:, at, :], GT.at[:, at, :], AZ0 + k, (dp, seq)).wait_recv()
        gi = co * 16 + xl * 8 + zf
        rcopy(GG.at[gi], GG.at[gi], BZ0 + k, (dp, seq)).wait_recv()

    def step(start, size, gstart, gsize, ostart, ogstart, sa, sb, dev):
        a = rcopy(GT.at[:, rows_at(start, size), :], GT.at[:, rows_at(start, size), :], sa, dev)
        b = rcopy(GG.at[pl.ds(gstart, gsize)], GG.at[pl.ds(gstart, gsize)], sb, dev)
        a.start()
        b.start()
        sends.append(a)
        sends.append(b)
        rcopy(GT.at[:, rows_at(ostart, size), :], GT.at[:, rows_at(ostart, size), :], sa, dev).wait_recv()
        rcopy(GG.at[pl.ds(ogstart, gsize)], GG.at[pl.ds(ogstart, gsize)], sb, dev).wait_recv()

    step(co * 256 + xl * 128, 128, co * 16 + xl * 8, 8,
         co * 256 + (1 - xl) * 128, co * 16 + (1 - xl) * 8, AX0, BX0, xlo_dev)
    step(co * 256, 256, co * 16, 16, (1 - co) * 256, (1 - co) * 16, AC0, BC0, core_dev)
    for j in range(8):
        for b in range(4):
            ghid[:, j * W + b * B:j * W + (b + 1) * B] = jnp.transpose(GT[j, b * B:(b + 1) * B, :])
    gg[...] = GG[:, 0, :]

    for c in hsend + msend + hc + sends + [dc, dx] + dz + dpc:
        c.wait_send()

    @pl.loop(0, CH)
    def _(c):
        s1(c).wait_send()
        s2(c).wait_send()
        sx(c).wait_send()
        gx(c).wait_send()
        g2(c).wait_send()
        g1(c).wait_send()
    for c in range(CH):
        head_copy(c).wait()


def fused(hidden, gain, head_weight, targets, loss_mask):
    wgt = jnp.pad(head_weight, ((0, CH * R - V), (0, 0)))
    vm = pl.BlockSpec(memory_space=pltpu.VMEM)
    scratch = [
        pltpu.VMEM((8, B, W), BF16),
        pltpu.VMEM((8, 8, B), F32),
        pltpu.VMEM((CH, W, R), BF16),
        pltpu.VMEM((CAP, 8 * B), BF16),
        pltpu.VMEM((8, 128), F32),
        pltpu.VMEM((W, CAP), F32),
        pltpu.VMEM((CAP, W), BF16),
        pltpu.VMEM((W, B), F32),
        pltpu.VMEM((8, CAP), F32),
        pltpu.VMEM((CH, R, CAP), BF16),
        pltpu.VMEM((CH, 192, CAP), BF16),
        pltpu.VMEM((CH, 192, CAP), BF16),
        pltpu.VMEM((CH, 96, CAP), BF16),
        pltpu.VMEM((CH, 96, CAP), BF16),
        pltpu.VMEM((CH, 48, CAP), BF16),
        pltpu.VMEM((CH, 48, CAP), F32),
        pltpu.VMEM((8, CAP), F32),
        pltpu.VMEM((4, 8, CAP), F32),
        pltpu.VMEM((8, 8, CAP), F32),
        pltpu.VMEM((8, 8, CAP), F32),
        pltpu.VMEM((CH, R, CAP), BF16),
        pltpu.VMEM((W, CAP), F32),
        pltpu.VMEM((256, CAP), F32),
        pltpu.VMEM((256, CAP), F32),
        pltpu.VMEM((128, CAP), BF16),
        pltpu.VMEM((128, CAP), BF16),
        pltpu.VMEM((128, CAP), F32),
        pltpu.VMEM((8, 16, CAP), BF16),
        pltpu.VMEM((8, 16, CAP), BF16),
        pltpu.VMEM((8, 32, B), BF16),
        pltpu.VMEM((8, 32, B), BF16),
        pltpu.VMEM((8, W, B), BF16),
        pltpu.VMEM((32, 8, B), F32),
        pltpu.VMEM((CH, R, W), F32),
        pltpu.SemaphoreType.DMA((NSEM,)),
        pltpu.SemaphoreType.DMA((NSEM,)),
        pltpu.SemaphoreType.DMA((CH,)),
    ]
    gh, ghid, gg, scal = pl.pallas_call(
        kernel,
        out_shape=(
            jax.ShapeDtypeStruct((V, W), F32),
            jax.ShapeDtypeStruct((B, D), BF16),
            jax.ShapeDtypeStruct((32, B), F32),
            jax.ShapeDtypeStruct((8, B), F32),
        ),
        in_specs=[vm] * 5,
        out_specs=(pl.BlockSpec(memory_space=pl.ANY), vm, vm, vm),
        scratch_shapes=scratch,
        compiler_params=pltpu.CompilerParams(
            collective_id=0, has_side_effects=True, vmem_limit_bytes=56 * 1024 * 1024),
        cost_estimate=pl.CostEstimate(flops=6 * V * CAP * W, bytes_accessed=16 * 1024 * 1024, transcendentals=0),
        name="fused",
    )(hidden, gain.reshape(8, W), wgt, targets.reshape(1, B), loss_mask.reshape(1, B))
    grad_gain = jnp.transpose(gg.reshape(32, 8, 16), (1, 0, 2)).reshape(D)
    return scal, ghid, grad_gain, gh


def norm_back(grad_normed, unit_rows, inv_rms, gain):
    grad_unit = grad_normed * gain
    return inv_rms * (
        grad_unit - unit_rows * jnp.mean(grad_unit * unit_rows, axis=-1, keepdims=True)
    )


def general(hidden, gain, head_weight, targets, loss_mask):
    floats = hidden.astype(jnp.float32)
    inv_rms = lax.rsqrt(jnp.mean(floats * floats, axis=-1, keepdims=True) + EPS)
    unit_rows = floats * inv_rms
    normed = (unit_rows * gain).astype(jnp.bfloat16)
    mask_float = loss_mask.astype(jnp.float32)
    num_valid = lax.psum(jnp.sum(mask_float), "dp")
    slices = lax.all_to_all(normed, "dp", split_axis=1, concat_axis=0, tiled=True)
    vocab_rows = head_weight.shape[0]
    logits = lax.psum_scatter(
        lax.dot_general(slices, head_weight, NT, preferred_element_type=jnp.float32),
        "dp",
        scatter_dimension=0,
        tiled=True,
    )
    column = lax.axis_index("seq") * vocab_rows + jnp.arange(vocab_rows, dtype=jnp.int32)
    one_hot = (column[None, :] == targets[:, None]).astype(jnp.float32)
    local_picked = jnp.sum(one_hot * logits, axis=1)
    row_top = lax.pmax(jnp.max(logits, axis=1), "seq")
    shifted = jnp.exp(logits - row_top[:, None])
    row_total, picked = lax.psum((jnp.sum(shifted, axis=1), local_picked), "seq")
    log_total = row_top + jnp.log(row_total)
    probs = shifted / row_total[:, None]
    row_loss = log_total - picked
    loss_value = lax.psum(jnp.sum(mask_float * row_loss), "dp") / num_valid
    dlogits = ((probs - one_hot) * (mask_float / num_valid)[:, None]).astype(jnp.bfloat16)
    shard_rows = lax.all_gather(dlogits, "dp", axis=0, tiled=True)
    grad_slices = jnp.dot(shard_rows, head_weight, preferred_element_type=jnp.float32)
    grad_head = lax.dot_general(
        shard_rows, slices, (((0,), (0,)), ((), ())), preferred_element_type=jnp.float32
    )
    returned = lax.all_to_all(grad_slices, "dp", split_axis=0, concat_axis=1, tiled=True)
    grad_normed = lax.psum(returned, "seq")
    grad_gain = lax.psum(jnp.sum(grad_normed * unit_rows, axis=0), "dp")
    grad_hidden = norm_back(grad_normed, unit_rows, inv_rms, gain).astype(jnp.bfloat16)
    return (loss_value, grad_hidden, grad_gain, grad_head)


def body(hidden, gain, head_weight, targets, loss_mask):
    scal, grad_hidden, grad_gain, grad_head = fused(hidden, gain, head_weight, targets, loss_mask)

    def keep(*args):
        return scal[0, 0], grad_hidden, grad_gain, grad_head

    return lax.cond(scal[1, 0] > 0.5, general, keep, hidden, gain, head_weight, targets, loss_mask)


def solution(mesh):
    return jax.shard_map(
        body,
        mesh=mesh,
        in_specs=(P("dp", None), P(), P("seq", "dp"), P("dp"), P("dp")),
        out_specs=(P(), P("dp", None), P(), P("seq", "dp")),
        check_vma=False,
    )
```

```python
import jax
import jax.numpy as jnp
from jax import lax
from jax.experimental import pallas as pl
from jax.experimental.pallas import tpu as pltpu
from jax.sharding import PartitionSpec as P

EPS = 1e-05
MESH = pl.DeviceIdType.MESH
F32 = jnp.float32
BF16 = jnp.bfloat16
NT = (((1,), (1,)), ((), ()))

D = 4096
W = 512
B = 128
V = 2632
VP = 2688
CAP = 640
CH = 7
R = VP // CH
RH, RQ, RP = R // 2, R // 4, R // 8
G = 384
LOW = -1e30

LAG1, LAG2, LAG3, LAG4, LAG5 = 2, 3, 4, 6, 8

NSEM = 0


def sems(n):
    global NSEM
    NSEM += n
    return NSEM - n


H0, M0, HC0 = sems(8), sems(8), sems(8)
S10, S20, S30, G30, G20, G10 = [sems(CH) for _ in range(6)]
T10, T20, T30 = sems(4), sems(8), sems(8)
DC0, DX0, DZ0, DP0, AZ0, AX0, AC0 = sems(1), sems(8), sems(8), sems(8), sems(8), sems(8), sems(2)


def kernel(hid, gain, wgt, tgt, msk, dlo, C, GTX, scal, flag,
           H, META, WP, WT, S, HCT, GCOL, ROWS, L, R1, A1, R2, A2, R3, STAT, ST1, ST2, ST3,
           PR, DN, RC, T1, B1, RX, B2, RZ, MB, RB, ss, rs):
    dp = lax.axis_index("dp")
    seq = lax.axis_index("seq")
    y, xh = dp // 2, dp % 2
    z, xl, co = seq // 4, (seq // 2) % 2, seq % 2
    p1, p2 = (y // 2 + y) % 2, y // 2
    ya, yb = (y + 1 - 2 * (y % 2)) * 2 + xh, (3 - y) * 2 + xh
    xpeer = y * 2 + 1 - xh

    def seq_of(zz, xx, cc):
        return zz * 4 + xx * 2 + cc

    def rcopy(src, dst, sem, dev):
        return pltpu.make_async_remote_copy(
            src_ref=src, dst_ref=dst, send_sem=ss.at[sem], recv_sem=rs.at[sem],
            device_id=dev, device_id_type=MESH)

    def rows_at(start, size):
        return pl.ds(pl.multiple_of(start, 16), size)

    dp_peers = [lax.rem(dp + k, 8) for k in range(1, 8)]
    dp_from = [lax.rem(dp + 8 - k, 8) for k in range(1, 8)]
    z_peers = [lax.rem(z + k, 8) for k in range(1, 8)]
    z_from = [lax.rem(z + 8 - k, 8) for k in range(1, 8)]
    g_me = xl * 2 + co
    g_peers = [lax.rem(g_me + k, 4) for k in range(1, 4)]
    g_from = [lax.rem(g_me + 4 - k, 4) for k in range(1, 4)]
    core_dev = (dp, seq_of(z, xl, 1 - co))
    xlo_dev = (dp, seq_of(z, 1 - xl, co))

    barrier = pltpu.get_barrier_semaphore()
    for j in dp_peers:
        pl.semaphore_signal(barrier, inc=1, device_id=(j, seq), device_id_type=MESH)
    for g in g_peers:
        pl.semaphore_signal(barrier, inc=1, device_id=(dp, z * 4 + g), device_id_type=MESH)
    for zz in z_peers:
        pl.semaphore_signal(barrier, inc=1, device_id=(dp, seq_of(zz, xl, co)), device_id_type=MESH)

    total = jnp.zeros((B, 1), F32)
    for j in range(8):
        x = hid[:, j * W:(j + 1) * W].astype(F32)
        total = total + jnp.sum(x * x, axis=1, keepdims=True)
    rinv = lax.rsqrt(total * (1.0 / D) + EPS)
    rinv_t = jnp.transpose(jnp.broadcast_to(rinv, (B, B)))
    META[dp] = jnp.concatenate(
        [rinv_t[0:1, :], msk[...].astype(F32), tgt[...].astype(F32), jnp.zeros((5, B), F32)], axis=0)
    H[dp] = hid[:, pl.ds(pl.multiple_of(dp * W, W), W)]
    pl.semaphore_wait(barrier, 17)

    half = pl.ds(pl.multiple_of(co * 64, 64), 64)
    ohalf = pl.ds(pl.multiple_of((1 - co) * 64, 64), 64)
    hsend = []
    msend = []
    for k in range(1, 8):
        j = dp_peers[k - 1]
        c = rcopy(META.at[dp], META.at[dp], M0 + k, (j, seq))
        c.start()
        msend.append(c)
        c = rcopy(hid.at[half, pl.ds(pl.multiple_of(j * W, W), W)], H.at[dp, half, :], H0 + k, (j, seq))
        c.start()
        hsend.append(c)

    for i in range(6):
        WP[i * G:(i + 1) * G, :] = wgt[i * G:(i + 1) * G, :]
    WP[6 * G:V - 8, :] = wgt[6 * G:V - 8, :]
    WP[V - 8:V + 8, :] = jnp.concatenate(
        [wgt[V - 8:V, :].astype(F32), jnp.zeros((8, W), F32)], axis=0).astype(BF16)
    WP[V + 8:VP, :] = jnp.zeros((VP - V - 8, W), BF16)
    gain_row = jnp.concatenate([gain[pl.ds(dp * 4 + i, 1), :] for i in range(4)], axis=1)
    GCOL[...] = jnp.transpose(jnp.broadcast_to(gain_row, (B, W)))
    STAT[...] = jnp.concatenate([jnp.full((1, CAP), LOW, F32), jnp.zeros((7, CAP), F32)], axis=0)
    DN[...] = jnp.zeros_like(DN)

    for k in range(1, 8):
        j = dp_from[k - 1]
        rcopy(META.at[j], META.at[j], M0 + k, (dp, seq)).wait_recv()
    metas = [META[j] for j in range(8)]
    m8 = jnp.concatenate([m[1:2, :] for m in metas] + [jnp.zeros((8, B), F32)], axis=0)
    tri = (lax.broadcasted_iota(jnp.int32, (B, B), 0) <= lax.broadcasted_iota(jnp.int32, (B, B), 1)).astype(F32)
    cum = jnp.dot(m8.astype(BF16), tri.astype(BF16), preferred_element_type=F32)
    base = jnp.zeros((1, 1), F32)
    slot = lax.broadcasted_iota(jnp.int32, (CAP, B), 0)
    for j in range(8):
        rank = jnp.where(metas[j][1:2, :] > 0.5, cum[j:j + 1, :] + base - 1.0, -1.0).astype(jnp.int32)
        S[:, j * B:(j + 1) * B] = (slot == rank).astype(F32).astype(BF16)
        base = base + jnp.sum(metas[j][1:2, :], axis=1, keepdims=True)
    count = base
    r_all = jnp.concatenate([m[0:1, :] for m in metas], axis=1)
    v_all = jnp.concatenate([m[1:2, :] for m in metas], axis=1)
    t_all = jnp.concatenate([m[2:3, :] for m in metas], axis=1)
    hi = r_all.astype(BF16).astype(F32)
    mid = (r_all - hi).astype(BF16).astype(F32)
    lo = (r_all - hi) - mid
    ta = jnp.floor(t_all * (1.0 / 4096))
    tb = jnp.floor((t_all - ta * 4096) * (1.0 / 64))
    tc = t_all - ta * 4096 - tb * 64
    mr = jnp.concatenate([hi, mid, lo, v_all, ta, tb, tc, jnp.zeros((9, 8 * B), F32)], axis=0).astype(BF16)
    crow = lax.dot_general(mr, S[...], NT, preferred_element_type=F32)
    mr2 = jnp.concatenate([mr, jnp.zeros((B - 16, 8 * B), BF16)], axis=0)
    ccol = lax.dot_general(S[...], mr2, NT, preferred_element_type=F32)
    valid_row = crow[3:4, :]
    tgt_f = crow[4:5, :] * 4096.0 + crow[5:6, :] * 64.0 + crow[6:7, :] - (seq * V).astype(F32)
    here = jnp.logical_and(valid_row > 0.5, jnp.logical_and(tgt_f > -0.5, tgt_f < V - 0.5))
    tgt_f = jnp.where(here, tgt_f, -1.0)
    rinv_col = ccol[:, 0:1] + ccol[:, 1:2] + ccol[:, 2:3]
    ROWS[...] = jnp.concatenate(
        [crow[0:1, :] + crow[1:2, :] + crow[2:3, :], valid_row / count, tgt_f, valid_row,
         jnp.zeros((4, CAP), F32)], axis=0)

    hc = []
    for k in range(1, 8):
        j = dp_from[k - 1]
        rcopy(H.at[j, half, :], H.at[j, half, :], H0 + k, (dp, seq)).wait_recv()
        c = rcopy(H.at[j, half, :], H.at[j, half, :], HC0 + k, core_dev)
        c.start()
        hc.append(c)
    for k in range(1, 8):
        j = dp_from[k - 1]
        rcopy(H.at[j, ohalf, :], H.at[j, ohalf, :], HC0 + k, core_dev).wait_recv()
    hcomp = jnp.dot(S[...], H[...].reshape(8 * B, W), preferred_element_type=F32)
    C[...] = ((hcomp * rinv_col) * gain_row).astype(BF16)

    def axis(c, s):
        a = (c + s) % 3
        e0, e1, e2 = (2 - a) * (1 - a) // 2, a * (2 - a), a * (a - 1) // 2
        return p1 * e0 + p2 * e1 + xh * e2, (ya * e0 + yb * e1 + xpeer * e2, seq)

    def bits(c):
        return axis(c, 0)[0], axis(c, 1)[0], axis(c, 2)[0]

    def s1(c):
        f, g, h = bits(c)
        return rcopy(L.at[rows_at(c * R + (1 - f) * RH, RH), :], R1.at[c], S10 + c, axis(c, 0)[1])

    def s2(c):
        f, g, h = bits(c)
        return rcopy(A1.at[c, rows_at((1 - g) * RQ, RQ), :], R2.at[c], S20 + c, axis(c, 1)[1])

    def s3(c):
        f, g, h = bits(c)
        return rcopy(A2.at[c, rows_at((1 - h) * RP, RP), :], R3.at[c], S30 + c, axis(c, 2)[1])

    def within(start, size, sem, dev):
        return rcopy(PR.at[rows_at(start, size), :], PR.at[rows_at(start, size), :], sem, dev)

    def g3(c, other=0):
        f, g, h = bits(c)
        h = h + other * (1 - 2 * h)
        return within(c * R + f * RH + g * RQ + h * RP, RP, G30 + c, axis(c, 2)[1])

    def g2(c, other=0):
        f, g, h = bits(c)
        g = g + other * (1 - 2 * g)
        return within(c * R + f * RH + g * RQ, RQ, G20 + c, axis(c, 1)[1])

    def g1(c, other=0):
        f, g, h = bits(c)
        f = f + other * (1 - 2 * f)
        return within(c * R + f * RH, RH, G10 + c, axis(c, 0)[1])

    def gather_steps(k):
        @pl.when(jnp.logical_and(k >= LAG4, k < CH + LAG4))
        def _():
            g3(k - LAG4, 1).wait_recv()
            g2(k - LAG4).start()

        @pl.when(jnp.logical_and(k >= LAG5, k < CH + LAG5))
        def _():
            g2(k - LAG5, 1).wait_recv()
            g1(k - LAG5).start()

    @pl.loop(0, CH + LAG3)
    def _(k):
        @pl.when(k < CH)
        def _():
            rows = rows_at(k * R, R)
            L[rows, :] = lax.dot_general(WP[rows, :], C[...], NT, preferred_element_type=F32).astype(BF16)
            s1(k).start()

        @pl.when(jnp.logical_and(k >= LAG1, k < CH + LAG1))
        def _():
            c = k - LAG1
            f, g, h = bits(c)
            s1(c).wait_recv()
            A1[c] = (L[rows_at(c * R + f * RH, RH), :].astype(F32) + R1[c].astype(F32)).astype(BF16)
            s2(c).start()

        @pl.when(jnp.logical_and(k >= LAG2, k < CH + LAG2))
        def _():
            c = k - LAG2
            f, g, h = bits(c)
            s2(c).wait_recv()
            A2[c] = (A1[c, rows_at(g * RQ, RQ), :].astype(F32) + R2[c].astype(F32)).astype(BF16)
            s3(c).start()

        @pl.when(k >= LAG3)
        def _():
            c = k - LAG3
            f, g, h = bits(c)
            s3(c).wait_recv()
            logits = A2[c, rows_at(h * RP, RP), :].astype(F32) + R3[c].astype(F32)
            first = c * R + f * RH + g * RQ + h * RP
            local = first + lax.broadcasted_iota(jnp.int32, (RP, CAP), 0)
            inside = local < V
            ex = jnp.where(inside, jnp.exp(logits), 0.0)
            PR[rows_at(first, RP), :] = ex.astype(BF16)
            g3(c).start()
            hit = local == ROWS[2:3, :].astype(jnp.int32)
            STAT[0:1, :] = jnp.maximum(
                STAT[0:1, :], jnp.max(jnp.where(inside, logits, LOW), axis=0, keepdims=True))
            STAT[1:2, :] = STAT[1:2, :] + jnp.sum(ex, axis=0, keepdims=True)
            STAT[2:3, :] = STAT[2:3, :] + jnp.sum(ex * logits, axis=0, keepdims=True)
            STAT[3:4, :] = STAT[3:4, :] + jnp.sum(jnp.where(hit, logits, 0.0), axis=0, keepdims=True)

        gather_steps(k)

    def merge(slots, n):
        parts = [slots[i] for i in range(n)]
        top = parts[0][0:1, :]
        sums = parts[0][1:4, :]
        for q in parts[1:]:
            top = jnp.maximum(top, q[0:1, :])
            sums = sums + q[1:4, :]
        return jnp.concatenate([top, sums, jnp.zeros((4, CAP), F32)], axis=0)

    sends = []

    def spread(slots, mine, devs, sem):
        for k, dev in enumerate(devs, 1):
            c = rcopy(slots.at[mine], slots.at[mine], sem + k, dev)
            c.start()
            sends.append(c)

    def collect(slots, froms, sem):
        for k, src in enumerate(froms, 1):
            rcopy(slots.at[src], slots.at[src], sem + k, (dp, seq)).wait_recv()

    last = CH + LAG3
    mids = [last + (LAG5 - LAG3) * i // 3 for i in range(4)]
    ST1[g_me] = STAT[...]
    spread(ST1, g_me, [(dp, z * 4 + g) for g in g_peers], T10)
    HCT[...] = jnp.transpose(hcomp)

    @pl.loop(mids[0], mids[1])
    def _(k):
        gather_steps(k)
    collect(ST1, g_from, T10)
    ST2[z] = merge(ST1, 4)
    spread(ST2, z, [(dp, seq_of(zz, xl, co)) for zz in z_peers], T20)

    @pl.loop(0, VP // G)
    def _(i):
        WT[i] = jnp.transpose(WP[pl.ds(pl.multiple_of(i * G, G), G), :])

    @pl.loop(mids[1], mids[2])
    def _(k):
        gather_steps(k)
    collect(ST2, z_from, T20)
    ST3[dp] = merge(ST2, 8)
    spread(ST3, dp, [(j, seq) for j in dp_peers], T30)

    @pl.loop(mids[2], mids[3])
    def _(k):
        gather_steps(k)
    collect(ST3, dp_from, T30)
    stat = merge(ST3, 8)
    top, ssum, esum, tsum = [stat[i:i + 1, :] for i in range(4)]
    share = ROWS[1:2, :]
    valid = ROWS[3:4, :] > 0.5
    loss = jnp.sum(jnp.where(valid, jnp.log(ssum) - tsum, 0.0), axis=1, keepdims=True) / count
    size = jnp.abs(top)
    peak = (1.0 + size) * jnp.exp(top) / ssum
    odd = jnp.where(jnp.logical_and(valid, jnp.logical_or(size > 40.0, peak > 0.25)), 1.0, 0.0)
    odd = jnp.maximum(jnp.max(odd, axis=1, keepdims=True), jnp.where(count > CAP + 0.5, 1.0, 0.0))
    scal[...] = loss
    flag[...] = odd.astype(jnp.int32)
    ROWS[4:5, :] = share / ssum
    ROWS[5:6, :] = (esum / ssum - tsum) * share * (1.0 / D)

    @pl.loop(0, VP // G)
    def _(i):
        for q in range(CH * G // VP):
            g1(i * (CH * G // VP) + q, 1).wait_recv()
        rows = rows_at(i * G, G)
        local = i * G + lax.broadcasted_iota(jnp.int32, (G, CAP), 0)
        hit = local == ROWS[2:3, :].astype(jnp.int32)
        dl = PR[rows, :].astype(F32) * ROWS[4:5, :] - jnp.where(hit, ROWS[1:2, :], 0.0)
        dlo[rows, :] = dl.astype(BF16)
        DN[...] += jnp.dot(WT[i], dlo[rows, :], preferred_element_type=F32)

    dc = rcopy(DN.at[rows_at((1 - co) * 256, 256), :], RC, DC0, core_dev)
    dc.start()
    dc.wait_recv()
    T1[...] = DN[rows_at(co * 256, 256), :] + RC[...]
    far = (4, 3, 5, 2, 6, 1, 7, 0)
    dx = []
    for n, k in enumerate(far):
        zz = lax.rem(z + k, 8)
        B1[zz] = T1[rows_at((1 - xl) * 128 + zz * 16, 16), :].astype(BF16)
        c = rcopy(B1.at[zz], RX.at[zz], DX0 + n, xlo_dev)
        c.start()
        dx.append(c)
    dz = []
    for n, k in enumerate(far):
        zz = lax.rem(z + k, 8)
        dx[n].wait_recv()
        part = T1[rows_at(xl * 128 + zz * 16, 16), :] + RX[zz].astype(F32)
        if k:
            B2[zz] = part.astype(BF16)
            c = rcopy(B2.at[zz], RZ.at[z], DZ0 + k, (dp, seq_of(zz, xl, co)))
            c.start()
            dz.append(c)
    dn = part
    for k in (1, 7, 2, 6, 3, 5, 4):
        rcopy(RZ.at[z_from[k - 1]], RZ.at[z_from[k - 1]], DZ0 + k, (dp, seq)).wait_recv()
        dn = dn + RZ[z_from[k - 1]].astype(F32)

    off = co * 256 + xl * 128 + z * 16
    rinv_row = ROWS[0:1, :]
    xn = HCT[rows_at(off, 16), :] * rinv_row
    gc = GCOL[rows_at(off, 16), 0:1]
    grow = (rinv_row * (dn * gc - xn * ROWS[5:6, :])).astype(BF16)
    ggc = jnp.sum(dn * xn, axis=1, keepdims=True)
    wide_rows = jnp.dot(grow, S[...], preferred_element_type=F32).astype(BF16)
    ghi = ggc.astype(BF16).astype(F32)
    gmid = (ggc - ghi).astype(BF16).astype(F32)
    glo = (ggc - ghi) - gmid
    lane = lax.broadcasted_iota(jnp.int32, (16, B), 1)
    gparts = jnp.where(lane == 0, ghi, jnp.where(lane == 1, gmid, jnp.where(lane == 2, glo, 0.0))).astype(BF16)
    for j in range(8):
        MB[j, 0:16, :] = wide_rows[:, j * B:(j + 1) * B]
        MB[j, 16:32, :] = gparts
    dpc = []
    for k in range(1, 8):
        c = rcopy(MB.at[dp_peers[k - 1]], RB.at[dp], DP0 + k, (dp_peers[k - 1], seq))
        c.start()
        dpc.append(c)
    RB[dp] = MB[dp]
    for k in range(1, 8):
        rcopy(RB.at[dp_from[k - 1]], RB.at[dp_from[k - 1]], DP0 + k, (dp, seq)).wait_recv()

    mine = co * 16 + xl * 8 + z
    GTX[mine, 0:B, :] = RB[:, 0:16, :].reshape(B, B)
    GTX[mine, B:B + 16, :] = jnp.transpose(RB[:, 16:32, :].reshape(B, B).astype(F32))[0:16, :].astype(BF16)

    def slice_copy(i, n, sem, dev):
        return rcopy(GTX.at[pl.ds(i, n)], GTX.at[pl.ds(i, n)], sem, dev)

    for k in (4, 3, 5, 2, 6, 1, 7):
        c = slice_copy(mine, 1, AZ0 + k, (dp, seq_of(z_peers[k - 1], xl, co)))
        c.start()
        sends.append(c)
    c = slice_copy(mine, 1, AX0, xlo_dev)
    c.start()
    sends.append(c)
    for k in (1, 7, 2, 6, 3, 5, 4):
        src = co * 16 + xl * 8 + z_from[k - 1]
        slice_copy(src, 1, AZ0 + k, (dp, seq)).wait_recv()
        c = slice_copy(src, 1, AX0 + k, xlo_dev)
        c.start()
        sends.append(c)
    c = slice_copy(co * 16 + xl * 8, 8, AC0, core_dev)
    c.start()
    sends.append(c)
    for k in (0, 1, 7, 2, 6, 3, 5, 4):
        src = co * 16 + (1 - xl) * 8 + (z_from[k - 1] if k else z)
        slice_copy(src, 1, AX0 + k, (dp, seq)).wait_recv()
    c = slice_copy(co * 16 + (1 - xl) * 8, 8, AC0 + 1, core_dev)
    c.start()
    sends.append(c)
    slice_copy((1 - co) * 16 + xl * 8, 8, AC0, core_dev).wait_recv()
    slice_copy((1 - co) * 16 + (1 - xl) * 8, 8, AC0 + 1, core_dev).wait_recv()

    for c in hsend + msend + hc + sends + [dc] + dx + dz + dpc:
        c.wait_send()

    @pl.loop(0, CH)
    def _(c):
        s1(c).wait_send()
        s2(c).wait_send()
        s3(c).wait_send()
        g3(c).wait_send()
        g2(c).wait_send()
        g1(c).wait_send()


def fused(hidden, gain, head_weight, targets, loss_mask):
    vm = pl.BlockSpec(memory_space=pltpu.VMEM)
    scratch = [
        pltpu.VMEM((8, B, W), BF16),
        pltpu.VMEM((8, 8, B), F32),
        pltpu.VMEM((VP, W), BF16),
        pltpu.VMEM((VP // G, W, G), BF16),
        pltpu.VMEM((CAP, 8 * B), BF16),
        pltpu.VMEM((W, CAP), F32),
        pltpu.VMEM((W, B), F32),
        pltpu.VMEM((8, CAP), F32),
        pltpu.VMEM((VP, CAP), BF16),
        pltpu.VMEM((CH, RH, CAP), BF16),
        pltpu.VMEM((CH, RH, CAP), BF16),
        pltpu.VMEM((CH, RQ, CAP), BF16),
        pltpu.VMEM((CH, RQ, CAP), BF16),
        pltpu.VMEM((CH, RP, CAP), BF16),
        pltpu.VMEM((8, CAP), F32),
        pltpu.VMEM((4, 8, CAP), F32),
        pltpu.VMEM((8, 8, CAP), F32),
        pltpu.VMEM((8, 8, CAP), F32),
        pltpu.VMEM((VP, CAP), BF16),
        pltpu.VMEM((W, CAP), F32),
        pltpu.VMEM((256, CAP), F32),
        pltpu.VMEM((256, CAP), F32),
        pltpu.VMEM((8, 16, CAP), BF16),
        pltpu.VMEM((8, 16, CAP), BF16),
        pltpu.VMEM((8, 16, CAP), BF16),
        pltpu.VMEM((8, 16, CAP), BF16),
        pltpu.VMEM((8, 32, B), BF16),
        pltpu.VMEM((8, 32, B), BF16),
        pltpu.SemaphoreType.DMA((NSEM,)),
        pltpu.SemaphoreType.DMA((NSEM,)),
    ]
    return pl.pallas_call(
        kernel,
        out_shape=(
            jax.ShapeDtypeStruct((VP, CAP), BF16),
            jax.ShapeDtypeStruct((CAP, W), BF16),
            jax.ShapeDtypeStruct((32, B + 16, B), BF16),
            jax.ShapeDtypeStruct((1, 1), F32),
            jax.ShapeDtypeStruct((1, 1), jnp.int32),
        ),
        in_specs=[vm] * 5,
        out_specs=(vm,) * 5,
        scratch_shapes=scratch,
        compiler_params=pltpu.CompilerParams(
            collective_id=0, has_side_effects=True, vmem_limit_bytes=44 * 1024 * 1024),
        cost_estimate=pl.CostEstimate(flops=6 * V * CAP * W, bytes_accessed=16 * 1024 * 1024, transcendentals=0),
        name="fused",
    )(hidden, gain.reshape(32, B), head_weight, targets.reshape(1, B), loss_mask.reshape(1, B))


STEPS = 8


def finish_kernel(dl, c, gtx, scal, gh, ghid, gg, loss):
    i = pl.program_id(0)
    n = VP // STEPS
    gh[...] = jnp.dot(dl[pl.ds(pl.multiple_of(i * n, 16), n), :], c[...], preferred_element_type=F32)
    block = gtx[:, pl.ds(pl.multiple_of(i * 16, 16), 16), :].reshape(W, B)
    ghid[...] = jnp.transpose(block)

    @pl.when(i == 0)
    def _():
        loss[...] = scal[...]
        parts = gtx[:, B:B + 16, :].astype(F32)
        sums = parts[:, 0, :] + parts[:, 1, :] + parts[:, 2, :]
        cols = jnp.transpose(jnp.concatenate([sums, jnp.zeros((B - 32, B), F32)], axis=0))
        row = lax.broadcasted_iota(jnp.int32, (B, B), 0)
        lane = lax.broadcasted_iota(jnp.int32, (B, B), 1)
        for q in range(4):
            pick = (row == q * 8 + lane // 16).astype(F32)
            spread = jnp.dot(cols, pick, precision=lax.Precision.HIGHEST, preferred_element_type=F32)
            spread = jnp.where(row % 16 == lane % 16, spread, 0.0)
            gg[:, q, :] = jnp.sum(spread.reshape(8, 16, B), axis=1)


def finish(dl, c, gtx, scal):
    vm = pl.BlockSpec(memory_space=pltpu.VMEM)
    n = VP // STEPS
    gh, ghid, gg, loss = pl.pallas_call(
        finish_kernel,
        grid=(STEPS,),
        out_shape=(
            jax.ShapeDtypeStruct((V, W), F32),
            jax.ShapeDtypeStruct((B, D), BF16),
            jax.ShapeDtypeStruct((8, 4, B), F32),
            jax.ShapeDtypeStruct((1, 1), F32),
        ),
        in_specs=[vm] * 4,
        out_specs=(
            pl.BlockSpec((n, W), lambda i: (i, 0)),
            pl.BlockSpec((B, W), lambda i: (0, i)),
            pl.BlockSpec((8, 4, B), lambda i: (0, 0, 0)),
            pl.BlockSpec((1, 1), lambda i: (0, 0)),
        ),
        compiler_params=pltpu.CompilerParams(vmem_limit_bytes=40 * 1024 * 1024),
        cost_estimate=pl.CostEstimate(flops=2 * V * CAP * W, bytes_accessed=8 * 1024 * 1024, transcendentals=0),
        name="finish",
    )(dl, c, gtx, scal)
    return loss.reshape(()), ghid, gg.reshape(D), gh


def norm_back(grad_normed, unit_rows, inv_rms, gain):
    grad_unit = grad_normed * gain
    return inv_rms * (
        grad_unit - unit_rows * jnp.mean(grad_unit * unit_rows, axis=-1, keepdims=True)
    )


def general(hidden, gain, head_weight, targets, loss_mask):
    floats = hidden.astype(jnp.float32)
    inv_rms = lax.rsqrt(jnp.mean(floats * floats, axis=-1, keepdims=True) + EPS)
    unit_rows = floats * inv_rms
    normed = (unit_rows * gain).astype(jnp.bfloat16)
    mask_float = loss_mask.astype(jnp.float32)
    num_valid = lax.psum(jnp.sum(mask_float), "dp")
    slices = lax.all_to_all(normed, "dp", split_axis=1, concat_axis=0, tiled=True)
    vocab_rows = head_weight.shape[0]
    logits = lax.psum_scatter(
        lax.dot_general(slices, head_weight, NT, preferred_element_type=jnp.float32),
        "dp",
        scatter_dimension=0,
        tiled=True,
    )
    column = lax.axis_index("seq") * vocab_rows + jnp.arange(vocab_rows, dtype=jnp.int32)
    one_hot = (column[None, :] == targets[:, None]).astype(jnp.float32)
    local_picked = jnp.sum(one_hot * logits, axis=1)
    row_top = lax.pmax(jnp.max(logits, axis=1), "seq")
    shifted = jnp.exp(logits - row_top[:, None])
    row_total, picked = lax.psum((jnp.sum(shifted, axis=1), local_picked), "seq")
    log_total = row_top + jnp.log(row_total)
    probs = shifted / row_total[:, None]
    row_loss = log_total - picked
    loss_value = lax.psum(jnp.sum(mask_float * row_loss), "dp") / num_valid
    dlogits = ((probs - one_hot) * (mask_float / num_valid)[:, None]).astype(jnp.bfloat16)
    shard_rows = lax.all_gather(dlogits, "dp", axis=0, tiled=True)
    grad_slices = jnp.dot(shard_rows, head_weight, preferred_element_type=jnp.float32)
    grad_head = lax.dot_general(
        shard_rows, slices, (((0,), (0,)), ((), ())), preferred_element_type=jnp.float32
    )
    returned = lax.all_to_all(grad_slices, "dp", split_axis=0, concat_axis=1, tiled=True)
    grad_normed = lax.psum(returned, "seq")
    grad_gain = lax.psum(jnp.sum(grad_normed * unit_rows, axis=0), "dp")
    grad_hidden = norm_back(grad_normed, unit_rows, inv_rms, gain).astype(jnp.bfloat16)
    return (loss_value, grad_hidden, grad_gain, grad_head)


def body(hidden, gain, head_weight, targets, loss_mask):
    dl, c, gtx, scal, flag = fused(hidden, gain, head_weight, targets, loss_mask)

    def fast(*args):
        return finish(dl, c, gtx, scal)

    return lax.cond(flag[0, 0] > 0, general, fast, hidden, gain, head_weight, targets, loss_mask)


def solution(mesh):
    return jax.shard_map(
        body,
        mesh=mesh,
        in_specs=(P("dp", None), P(), P("seq", "dp"), P("dp"), P("dp")),
        out_specs=(P(), P("dp", None), P(), P("seq", "dp")),
        check_vma=False,
    )
```

```python
import jax
import jax.numpy as jnp
from jax import lax
from jax.experimental import pallas as pl
from jax.experimental.pallas import tpu as pltpu
from jax.sharding import PartitionSpec as P

EPS = 1e-05
MESH = pl.DeviceIdType.MESH
F32 = jnp.float32
BF16 = jnp.bfloat16
NT = (((1,), (1,)), ((), ()))

D = 4096
W = 512
B = 128
V = 2632
VP = 2688
CAP = 640
CH = 21
R = VP // CH
RH, RQ, RP = R // 2, R // 4, R // 8
G = 384
LOW = -1e30

LAG1, LAG2, LAG3, LAG4, LAG5 = 8, 14, 20, 28, 36

NSEM = 0


def sems(n):
    global NSEM
    NSEM += n
    return NSEM - n


H0, M0, HC0 = sems(8), sems(8), sems(8)
S10, S20, S30, G30, G20, G10 = [sems(CH) for _ in range(6)]
T10, T20, T30 = sems(4), sems(8), sems(8)
DC0, DX0, DZ0, DP0, AZ0, AX0, AC0 = sems(1), sems(8), sems(8), sems(8), sems(8), sems(8), sems(16)


def kernel(hid_in, gain, wgt_in, tgt, msk, dlo, C, ghid, gg, scal, flag,
           hid, wgt, GTX, H, META, WP, WT, S, HCT, GCOL, ROWS, L, R1, A1, R2, A2, R3, STAT, ST1, ST2, ST3,
           PR, DN, RC, T1, B1, RX, B2, RZ, MB, RB, ss, rs, ls):
    dp = lax.axis_index("dp")
    seq = lax.axis_index("seq")
    y, xh = dp // 2, dp % 2
    z, xl, co = seq // 4, (seq // 2) % 2, seq % 2
    p1, p2 = (y // 2 + y) % 2, y // 2
    ya, yb = (y + 1 - 2 * (y % 2)) * 2 + xh, (3 - y) * 2 + xh
    xpeer = y * 2 + 1 - xh

    def seq_of(zz, xx, cc):
        return zz * 4 + xx * 2 + cc

    def rcopy(src, dst, sem, dev):
        return pltpu.make_async_remote_copy(
            src_ref=src, dst_ref=dst, send_sem=ss.at[sem], recv_sem=rs.at[sem],
            device_id=dev, device_id_type=MESH)

    def rows_at(start, size):
        return pl.ds(pl.multiple_of(start, 16), size)

    dp_peers = [lax.rem(dp + k, 8) for k in range(1, 8)]
    dp_from = [lax.rem(dp + 8 - k, 8) for k in range(1, 8)]
    z_peers = [lax.rem(z + k, 8) for k in range(1, 8)]
    z_from = [lax.rem(z + 8 - k, 8) for k in range(1, 8)]
    g_me = xl * 2 + co
    g_peers = [lax.rem(g_me + k, 4) for k in range(1, 4)]
    g_from = [lax.rem(g_me + 4 - k, 4) for k in range(1, 4)]
    core_dev = (dp, seq_of(z, xl, 1 - co))
    xlo_dev = (dp, seq_of(z, 1 - xl, co))

    fetch_hid = pltpu.make_async_copy(hid_in, hid, ls.at[0])
    fetch_hid.start()
    fetch_wgt = pltpu.make_async_copy(wgt_in, wgt, ls.at[1])
    fetch_wgt.start()

    barrier = pltpu.get_barrier_semaphore()
    for j in dp_peers:
        pl.semaphore_signal(barrier, inc=1, device_id=(j, seq), device_id_type=MESH)
    for g in g_peers:
        pl.semaphore_signal(barrier, inc=1, device_id=(dp, z * 4 + g), device_id_type=MESH)
    for zz in z_peers:
        pl.semaphore_signal(barrier, inc=1, device_id=(dp, seq_of(zz, xl, co)), device_id_type=MESH)

    fetch_hid.wait()
    total = jnp.zeros((B, 1), F32)
    for j in range(8):
        x = hid[:, j * W:(j + 1) * W].astype(F32)
        total = total + jnp.sum(x * x, axis=1, keepdims=True)
    rinv = lax.rsqrt(total * (1.0 / D) + EPS)
    rinv_t = jnp.transpose(jnp.broadcast_to(rinv, (B, B)))
    META[dp] = jnp.concatenate(
        [rinv_t[0:1, :], msk[...].astype(F32), tgt[...].astype(F32), jnp.zeros((5, B), F32)], axis=0)
    H[dp] = hid[:, pl.ds(pl.multiple_of(dp * W, W), W)]
    pl.semaphore_wait(barrier, 17)

    half = pl.ds(pl.multiple_of(co * 64, 64), 64)
    ohalf = pl.ds(pl.multiple_of((1 - co) * 64, 64), 64)
    hsend = []
    msend = []
    for k in range(1, 8):
        j = dp_peers[k - 1]
        c = rcopy(META.at[dp], META.at[dp], M0 + k, (j, seq))
        c.start()
        msend.append(c)
        c = rcopy(hid.at[half, pl.ds(pl.multiple_of(j * W, W), W)], H.at[dp, half, :], H0 + k, (j, seq))
        c.start()
        hsend.append(c)

    fetch_wgt.wait()
    for i in range(6):
        WP[i * G:(i + 1) * G, :] = wgt[i * G:(i + 1) * G, :]
    WP[6 * G:V - 8, :] = wgt[6 * G:V - 8, :]
    WP[V - 8:V + 8, :] = jnp.concatenate(
        [wgt[V - 8:V, :].astype(F32), jnp.zeros((8, W), F32)], axis=0).astype(BF16)
    WP[V + 8:VP, :] = jnp.zeros((VP - V - 8, W), BF16)
    gain_row = jnp.concatenate([gain[pl.ds(dp * 4 + i, 1), :] for i in range(4)], axis=1)
    GCOL[...] = jnp.transpose(jnp.broadcast_to(gain_row, (B, W)))
    STAT[...] = jnp.concatenate([jnp.full((1, CAP), LOW, F32), jnp.zeros((7, CAP), F32)], axis=0)
    DN[...] = jnp.zeros_like(DN)

    for k in range(1, 8):
        j = dp_from[k - 1]
        rcopy(META.at[j], META.at[j], M0 + k, (dp, seq)).wait_recv()
    metas = [META[j] for j in range(8)]
    m8 = jnp.concatenate([m[1:2, :] for m in metas] + [jnp.zeros((8, B), F32)], axis=0)
    tri = (lax.broadcasted_iota(jnp.int32, (B, B), 0) <= lax.broadcasted_iota(jnp.int32, (B, B), 1)).astype(F32)
    cum = jnp.dot(m8.astype(BF16), tri.astype(BF16), preferred_element_type=F32)
    base = jnp.zeros((1, 1), F32)
    slot = lax.broadcasted_iota(jnp.int32, (CAP, B), 0)
    for j in range(8):
        rank = jnp.where(metas[j][1:2, :] > 0.5, cum[j:j + 1, :] + base - 1.0, -1.0).astype(jnp.int32)
        S[:, j * B:(j + 1) * B] = (slot == rank).astype(F32).astype(BF16)
        base = base + jnp.sum(metas[j][1:2, :], axis=1, keepdims=True)
    count = base
    r_all = jnp.concatenate([m[0:1, :] for m in metas], axis=1)
    v_all = jnp.concatenate([m[1:2, :] for m in metas], axis=1)
    t_all = jnp.concatenate([m[2:3, :] for m in metas], axis=1)
    hi = r_all.astype(BF16).astype(F32)
    mid = (r_all - hi).astype(BF16).astype(F32)
    lo = (r_all - hi) - mid
    ta = jnp.floor(t_all * (1.0 / 4096))
    tb = jnp.floor((t_all - ta * 4096) * (1.0 / 64))
    tc = t_all - ta * 4096 - tb * 64
    mr = jnp.concatenate([hi, mid, lo, v_all, ta, tb, tc, jnp.zeros((9, 8 * B), F32)], axis=0).astype(BF16)
    crow = lax.dot_general(mr, S[...], NT, preferred_element_type=F32)
    mr2 = jnp.concatenate([mr, jnp.zeros((B - 16, 8 * B), BF16)], axis=0)
    ccol = lax.dot_general(S[...], mr2, NT, preferred_element_type=F32)
    valid_row = crow[3:4, :]
    tgt_f = crow[4:5, :] * 4096.0 + crow[5:6, :] * 64.0 + crow[6:7, :] - (seq * V).astype(F32)
    here = jnp.logical_and(valid_row > 0.5, jnp.logical_and(tgt_f > -0.5, tgt_f < V - 0.5))
    tgt_f = jnp.where(here, tgt_f, -1.0)
    rinv_col = ccol[:, 0:1] + ccol[:, 1:2] + ccol[:, 2:3]
    ROWS[...] = jnp.concatenate(
        [crow[0:1, :] + crow[1:2, :] + crow[2:3, :], valid_row / count, tgt_f, valid_row,
         jnp.zeros((4, CAP), F32)], axis=0)

    hc = []
    for k in range(1, 8):
        j = dp_from[k - 1]
        rcopy(H.at[j, half, :], H.at[j, half, :], H0 + k, (dp, seq)).wait_recv()
        c = rcopy(H.at[j, half, :], H.at[j, half, :], HC0 + k, core_dev)
        c.start()
        hc.append(c)
    for k in range(1, 8):
        j = dp_from[k - 1]
        rcopy(H.at[j, ohalf, :], H.at[j, ohalf, :], HC0 + k, core_dev).wait_recv()
    hcomp = jnp.dot(S[...], H[...].reshape(8 * B, W), preferred_element_type=F32)
    C[...] = ((hcomp * rinv_col) * gain_row).astype(BF16)

    def axis(c, s):
        a = (c + s) % 3
        e0, e1, e2 = (2 - a) * (1 - a) // 2, a * (2 - a), a * (a - 1) // 2
        return p1 * e0 + p2 * e1 + xh * e2, (ya * e0 + yb * e1 + xpeer * e2, seq)

    def bits(c):
        return axis(c, 0)[0], axis(c, 1)[0], axis(c, 2)[0]

    def s1(c):
        f, g, h = bits(c)
        return rcopy(L.at[rows_at(c * R + (1 - f) * RH, RH), :], R1.at[c], S10 + c, axis(c, 0)[1])

    def s2(c):
        f, g, h = bits(c)
        return rcopy(A1.at[c, rows_at((1 - g) * RQ, RQ), :], R2.at[c], S20 + c, axis(c, 1)[1])

    def s3(c):
        f, g, h = bits(c)
        return rcopy(A2.at[c, rows_at((1 - h) * RP, RP), :], R3.at[c], S30 + c, axis(c, 2)[1])

    def within(start, size, sem, dev):
        return rcopy(PR.at[rows_at(start, size), :], PR.at[rows_at(start, size), :], sem, dev)

    def g3(c, other=0):
        f, g, h = bits(c)
        h = h + other * (1 - 2 * h)
        return within(c * R + f * RH + g * RQ + h * RP, RP, G30 + c, axis(c, 2)[1])

    def g2(c, other=0):
        f, g, h = bits(c)
        g = g + other * (1 - 2 * g)
        return within(c * R + f * RH + g * RQ, RQ, G20 + c, axis(c, 1)[1])

    def g1(c, other=0):
        f, g, h = bits(c)
        f = f + other * (1 - 2 * f)
        return within(c * R + f * RH, RH, G10 + c, axis(c, 0)[1])

    def gather_steps(k):
        @pl.when(jnp.logical_and(k >= LAG4, k < CH + LAG4))
        def _():
            g3(k - LAG4, 1).wait_recv()
            g2(k - LAG4).start()

        @pl.when(jnp.logical_and(k >= LAG5, k < CH + LAG5))
        def _():
            g2(k - LAG5, 1).wait_recv()
            g1(k - LAG5).start()

    @pl.loop(0, CH + LAG3)
    def _(k):
        @pl.when(k < CH)
        def _():
            rows = rows_at(k * R, R)
            L[rows, :] = lax.dot_general(WP[rows, :], C[...], NT, preferred_element_type=F32).astype(BF16)
            s1(k).start()

        @pl.when(jnp.logical_and(k >= LAG1, k < CH + LAG1))
        def _():
            c = k - LAG1
            f, g, h = bits(c)
            s1(c).wait_recv()
            A1[c] = (L[rows_at(c * R + f * RH, RH), :].astype(F32) + R1[c].astype(F32)).astype(BF16)
            s2(c).start()

        @pl.when(jnp.logical_and(k >= LAG2, k < CH + LAG2))
        def _():
            c = k - LAG2
            f, g, h = bits(c)
            s2(c).wait_recv()
            A2[c] = (A1[c, rows_at(g * RQ, RQ), :].astype(F32) + R2[c].astype(F32)).astype(BF16)
            s3(c).start()

        @pl.when(k >= LAG3)
        def _():
            c = k - LAG3
            f, g, h = bits(c)
            s3(c).wait_recv()
            logits = A2[c, rows_at(h * RP, RP), :].astype(F32) + R3[c].astype(F32)
            first = c * R + f * RH + g * RQ + h * RP
            local = first + lax.broadcasted_iota(jnp.int32, (RP, CAP), 0)
            inside = local < V
            ex = jnp.where(inside, jnp.exp(logits), 0.0)
            PR[rows_at(first, RP), :] = ex.astype(BF16)
            g3(c).start()
            hit = local == ROWS[2:3, :].astype(jnp.int32)
            STAT[0:1, :] = jnp.maximum(
                STAT[0:1, :], jnp.max(jnp.where(inside, logits, LOW), axis=0, keepdims=True))
            STAT[1:2, :] = STAT[1:2, :] + jnp.sum(ex, axis=0, keepdims=True)
            STAT[2:3, :] = STAT[2:3, :] + jnp.sum(ex * logits, axis=0, keepdims=True)
            STAT[3:4, :] = STAT[3:4, :] + jnp.sum(jnp.where(hit, logits, 0.0), axis=0, keepdims=True)

        gather_steps(k)

    def merge(slots, n):
        parts = [slots[i] for i in range(n)]
        top = parts[0][0:1, :]
        sums = parts[0][1:4, :]
        for q in parts[1:]:
            top = jnp.maximum(top, q[0:1, :])
            sums = sums + q[1:4, :]
        return jnp.concatenate([top, sums, jnp.zeros((4, CAP), F32)], axis=0)

    sends = []

    def spread(slots, mine, devs, sem):
        for k, dev in enumerate(devs, 1):
            c = rcopy(slots.at[mine], slots.at[mine], sem + k, dev)
            c.start()
            sends.append(c)

    def collect(slots, froms, sem):
        for k, src in enumerate(froms, 1):
            rcopy(slots.at[src], slots.at[src], sem + k, (dp, seq)).wait_recv()

    last = CH + LAG3
    mids = [last + (LAG5 - LAG3) * i // 3 for i in range(4)]
    ST1[g_me] = STAT[...]
    spread(ST1, g_me, [(dp, z * 4 + g) for g in g_peers], T10)
    HCT[...] = jnp.transpose(hcomp)

    @pl.loop(mids[0], mids[1])
    def _(k):
        gather_steps(k)
    collect(ST1, g_from, T10)
    ST2[z] = merge(ST1, 4)
    spread(ST2, z, [(dp, seq_of(zz, xl, co)) for zz in z_peers], T20)

    @pl.loop(0, VP // G)
    def _(i):
        WT[i] = jnp.transpose(WP[pl.ds(pl.multiple_of(i * G, G), G), :])

    @pl.loop(mids[1], mids[2])
    def _(k):
        gather_steps(k)
    collect(ST2, z_from, T20)
    ST3[dp] = merge(ST2, 8)
    spread(ST3, dp, [(j, seq) for j in dp_peers], T30)

    @pl.loop(mids[2], mids[3])
    def _(k):
        gather_steps(k)
    collect(ST3, dp_from, T30)
    stat = merge(ST3, 8)
    top, ssum, esum, tsum = [stat[i:i + 1, :] for i in range(4)]
    share = ROWS[1:2, :]
    valid = ROWS[3:4, :] > 0.5
    loss = jnp.sum(jnp.where(valid, jnp.log(ssum) - tsum, 0.0), axis=1, keepdims=True) / count
    size = jnp.abs(top)
    peak = (1.0 + size) * jnp.exp(top) / ssum
    odd = jnp.where(jnp.logical_and(valid, jnp.logical_or(size > 40.0, peak > 0.25)), 1.0, 0.0)
    odd = jnp.maximum(jnp.max(odd, axis=1, keepdims=True), jnp.where(count > CAP + 0.5, 1.0, 0.0))
    scal[...] = loss
    flag[...] = odd.astype(jnp.int32)
    ROWS[4:5, :] = share / ssum
    ROWS[5:6, :] = (esum / ssum - tsum) * share * (1.0 / D)

    @pl.loop(0, VP // G)
    def _(i):
        for q in range(CH * G // VP):
            g1(i * (CH * G // VP) + q, 1).wait_recv()
        rows = rows_at(i * G, G)
        local = i * G + lax.broadcasted_iota(jnp.int32, (G, CAP), 0)
        hit = local == ROWS[2:3, :].astype(jnp.int32)
        dl = PR[rows, :].astype(F32) * ROWS[4:5, :] - jnp.where(hit, ROWS[1:2, :], 0.0)
        dlo[rows, :] = dl.astype(BF16)
        DN[...] += jnp.dot(WT[i], dlo[rows, :], preferred_element_type=F32)

    dc = rcopy(DN.at[rows_at((1 - co) * 256, 256), :], RC, DC0, core_dev)
    dc.start()
    dc.wait_recv()
    T1[...] = DN[rows_at(co * 256, 256), :] + RC[...]
    far = (4, 3, 5, 2, 6, 1, 7, 0)
    dx = []
    for n, k in enumerate(far):
        zz = lax.rem(z + k, 8)
        B1[zz] = T1[rows_at((1 - xl) * 128 + zz * 16, 16), :].astype(BF16)
        c = rcopy(B1.at[zz], RX.at[zz], DX0 + n, xlo_dev)
        c.start()
        dx.append(c)
    dz = []
    for n, k in enumerate(far):
        zz = lax.rem(z + k, 8)
        dx[n].wait_recv()
        part = T1[rows_at(xl * 128 + zz * 16, 16), :] + RX[zz].astype(F32)
        if k:
            B2[zz] = part.astype(BF16)
            c = rcopy(B2.at[zz], RZ.at[z], DZ0 + k, (dp, seq_of(zz, xl, co)))
            c.start()
            dz.append(c)
    dn = part
    for k in (1, 7, 2, 6, 3, 5, 4):
        rcopy(RZ.at[z_from[k - 1]], RZ.at[z_from[k - 1]], DZ0 + k, (dp, seq)).wait_recv()
        dn = dn + RZ[z_from[k - 1]].astype(F32)

    off = co * 256 + xl * 128 + z * 16
    rinv_row = ROWS[0:1, :]
    xn = HCT[rows_at(off, 16), :] * rinv_row
    gc = GCOL[rows_at(off, 16), 0:1]
    grow = (rinv_row * (dn * gc - xn * ROWS[5:6, :])).astype(BF16)
    ggc = jnp.sum(dn * xn, axis=1, keepdims=True)
    wide_rows = jnp.dot(grow, S[...], preferred_element_type=F32).astype(BF16)
    ghi = ggc.astype(BF16).astype(F32)
    gmid = (ggc - ghi).astype(BF16).astype(F32)
    glo = (ggc - ghi) - gmid
    lane = lax.broadcasted_iota(jnp.int32, (16, B), 1)
    gparts = jnp.where(lane == 0, ghi, jnp.where(lane == 1, gmid, jnp.where(lane == 2, glo, 0.0))).astype(BF16)
    for j in range(8):
        MB[j, 0:16, :] = wide_rows[:, j * B:(j + 1) * B]
        MB[j, 16:32, :] = gparts
    dpc = []
    for k in range(1, 8):
        c = rcopy(MB.at[dp_peers[k - 1]], RB.at[dp], DP0 + k, (dp_peers[k - 1], seq))
        c.start()
        dpc.append(c)
    RB[dp] = MB[dp]
    for k in range(1, 8):
        rcopy(RB.at[dp_from[k - 1]], RB.at[dp_from[k - 1]], DP0 + k, (dp, seq)).wait_recv()

    mine = co * 16 + xl * 8 + z
    GTX[mine, 0:B, :] = RB[:, 0:16, :].reshape(B, B)
    GTX[mine, B:B + 16, :] = jnp.transpose(RB[:, 16:32, :].reshape(B, B).astype(F32))[0:16, :].astype(BF16)

    def slice_copy(i, sem, dev):
        return rcopy(GTX.at[i], GTX.at[i], sem, dev)

    def forward(i, sem, dev):
        c = slice_copy(i, sem, dev)
        c.start()
        sends.append(c)

    row = lax.broadcasted_iota(jnp.int32, (B, B), 0)
    lane = lax.broadcasted_iota(jnp.int32, (B, B), 1)
    pick = (row == lane // 16).astype(F32)
    diag = row % 16 == lane % 16

    def emit(cc, xx):
        q = cc * 2 + xx
        at = pl.ds(q * 8, 8)
        for j in range(8):
            block = GTX[at, j * 16:(j + 1) * 16, :].reshape(B, B)
            ghid[:, pl.ds(pl.multiple_of(j * W + q * B, B), B)] = jnp.transpose(block)
        parts = GTX[at, B:B + 16, :].astype(F32)
        sums = parts[:, 0, :] + parts[:, 1, :] + parts[:, 2, :]
        cols = jnp.transpose(jnp.concatenate([sums, jnp.zeros((B - 8, B), F32)], axis=0))
        spread = jnp.dot(cols, pick, precision=lax.Precision.HIGHEST, preferred_element_type=F32)
        spread = jnp.sum(jnp.where(diag, spread, 0.0).reshape(8, 16, B), axis=1)
        for j in range(8):
            gg[pl.ds(j * 4 + q, 1), :] = spread[j:j + 1, :]

    near = (1, 7, 2, 6, 3, 5, 4)
    ox, oc = 1 - xl, 1 - co
    for k in (4, 3, 5, 2, 6, 1, 7):
        forward(mine, AZ0 + k, (dp, seq_of(z_peers[k - 1], xl, co)))
    forward(mine, AX0, xlo_dev)
    forward(mine, AC0, core_dev)
    for k in near:
        src = co * 16 + xl * 8 + z_from[k - 1]
        slice_copy(src, AZ0 + k, (dp, seq)).wait_recv()
        forward(src, AX0 + k, xlo_dev)
        forward(src, AC0 + k, core_dev)
    emit(co, xl)
    for k in (0,) + near:
        src = co * 16 + ox * 8 + (z_from[k - 1] if k else z)
        slice_copy(src, AX0 + k, (dp, seq)).wait_recv()
        forward(src, AC0 + 8 + k, core_dev)
    emit(co, ox)
    for k in (0,) + near:
        slice_copy(oc * 16 + xl * 8 + (z_from[k - 1] if k else z), AC0 + k, (dp, seq)).wait_recv()
    emit(oc, xl)
    for k in (0,) + near:
        slice_copy(oc * 16 + ox * 8 + (z_from[k - 1] if k else z), AC0 + 8 + k, (dp, seq)).wait_recv()
    emit(oc, ox)

    for c in hsend + msend + hc + sends + [dc] + dx + dz + dpc:
        c.wait_send()

    @pl.loop(0, CH)
    def _(c):
        s1(c).wait_send()
        s2(c).wait_send()
        s3(c).wait_send()
        g3(c).wait_send()
        g2(c).wait_send()
        g1(c).wait_send()


def fused(hidden, gain, head_weight, targets, loss_mask):
    vm = pl.BlockSpec(memory_space=pltpu.VMEM)
    hbm = pl.BlockSpec(memory_space=pl.ANY)
    scratch = [
        pltpu.VMEM((B, D), BF16),
        pltpu.VMEM((V, W), BF16),
        pltpu.VMEM((32, B + 16, B), BF16),
        pltpu.VMEM((8, B, W), BF16),
        pltpu.VMEM((8, 8, B), F32),
        pltpu.VMEM((VP, W), BF16),
        pltpu.VMEM((VP // G, W, G), BF16),
        pltpu.VMEM((CAP, 8 * B), BF16),
        pltpu.VMEM((W, CAP), F32),
        pltpu.VMEM((W, B), F32),
        pltpu.VMEM((8, CAP), F32),
        pltpu.VMEM((VP, CAP), BF16),
        pltpu.VMEM((CH, RH, CAP), BF16),
        pltpu.VMEM((CH, RH, CAP), BF16),
        pltpu.VMEM((CH, RQ, CAP), BF16),
        pltpu.VMEM((CH, RQ, CAP), BF16),
        pltpu.VMEM((CH, RP, CAP), BF16),
        pltpu.VMEM((8, CAP), F32),
        pltpu.VMEM((4, 8, CAP), F32),
        pltpu.VMEM((8, 8, CAP), F32),
        pltpu.VMEM((8, 8, CAP), F32),
        pltpu.VMEM((VP, CAP), BF16),
        pltpu.VMEM((W, CAP), F32),
        pltpu.VMEM((256, CAP), F32),
        pltpu.VMEM((256, CAP), F32),
        pltpu.VMEM((8, 16, CAP), BF16),
        pltpu.VMEM((8, 16, CAP), BF16),
        pltpu.VMEM((8, 16, CAP), BF16),
        pltpu.VMEM((8, 16, CAP), BF16),
        pltpu.VMEM((8, 32, B), BF16),
        pltpu.VMEM((8, 32, B), BF16),
        pltpu.SemaphoreType.DMA((NSEM,)),
        pltpu.SemaphoreType.DMA((NSEM,)),
        pltpu.SemaphoreType.DMA((2,)),
    ]
    return pl.pallas_call(
        kernel,
        out_shape=(
            jax.ShapeDtypeStruct((VP, CAP), BF16),
            jax.ShapeDtypeStruct((CAP, W), BF16),
            jax.ShapeDtypeStruct((B, D), BF16),
            jax.ShapeDtypeStruct((32, B), F32),
            jax.ShapeDtypeStruct((1, 1), F32),
            jax.ShapeDtypeStruct((1, 1), jnp.int32),
        ),
        in_specs=[hbm, vm, hbm, vm, vm],
        out_specs=(vm,) * 6,
        scratch_shapes=scratch,
        compiler_params=pltpu.CompilerParams(
            collective_id=0, has_side_effects=True, vmem_limit_bytes=44 * 1024 * 1024),
        cost_estimate=pl.CostEstimate(flops=6 * V * CAP * W, bytes_accessed=16 * 1024 * 1024, transcendentals=0),
        name="fused",
    )(hidden, gain.reshape(32, B), head_weight, targets.reshape(1, B), loss_mask.reshape(1, B))


STEPS = 8


def finish_kernel(dl, c, ghid, gg, scal, gh, ghid_out, gg_out, loss, fs):
    i = pl.program_id(0)
    n = VP // STEPS
    rows = pltpu.make_async_copy(ghid, ghid_out, fs.at[0])

    @pl.when(i == 0)
    def _():
        rows.start()
        gg_out[...] = gg[...]
        loss[...] = scal[...]

    gh[...] = jnp.dot(dl[pl.ds(pl.multiple_of(i * n, 16), n), :], c[...], preferred_element_type=F32)

    @pl.when(i == STEPS - 1)
    def _():
        rows.wait()


def finish(dl, c, ghid, gg, scal):
    vm = pl.BlockSpec(memory_space=pltpu.VMEM)
    n = VP // STEPS
    return pl.pallas_call(
        finish_kernel,
        grid=(STEPS,),
        out_shape=(
            jax.ShapeDtypeStruct((V, W), F32),
            jax.ShapeDtypeStruct((B, D), BF16),
            jax.ShapeDtypeStruct((32, B), F32),
            jax.ShapeDtypeStruct((1, 1), F32),
        ),
        in_specs=[vm] * 5,
        out_specs=(
            pl.BlockSpec((n, W), lambda i: (i, 0)),
            pl.BlockSpec(memory_space=pltpu.HBM),
            pl.BlockSpec((32, B), lambda i: (0, 0)),
            pl.BlockSpec((1, 1), lambda i: (0, 0)),
        ),
        scratch_shapes=[pltpu.SemaphoreType.DMA((1,))],
        compiler_params=pltpu.CompilerParams(vmem_limit_bytes=40 * 1024 * 1024),
        cost_estimate=pl.CostEstimate(flops=2 * V * CAP * W, bytes_accessed=8 * 1024 * 1024, transcendentals=0),
        name="finish",
    )(dl, c, ghid, gg, scal)


def norm_back(grad_normed, unit_rows, inv_rms, gain):
    grad_unit = grad_normed * gain
    return inv_rms * (
        grad_unit - unit_rows * jnp.mean(grad_unit * unit_rows, axis=-1, keepdims=True)
    )


def general(hidden, gain, head_weight, targets, loss_mask):
    floats = hidden.astype(jnp.float32)
    inv_rms = lax.rsqrt(jnp.mean(floats * floats, axis=-1, keepdims=True) + EPS)
    unit_rows = floats * inv_rms
    normed = (unit_rows * gain).astype(jnp.bfloat16)
    mask_float = loss_mask.astype(jnp.float32)
    num_valid = lax.psum(jnp.sum(mask_float), "dp")
    slices = lax.all_to_all(normed, "dp", split_axis=1, concat_axis=0, tiled=True)
    vocab_rows = head_weight.shape[0]
    logits = lax.psum_scatter(
        lax.dot_general(slices, head_weight, NT, preferred_element_type=jnp.float32),
        "dp",
        scatter_dimension=0,
        tiled=True,
    )
    column = lax.axis_index("seq") * vocab_rows + jnp.arange(vocab_rows, dtype=jnp.int32)
    one_hot = (column[None, :] == targets[:, None]).astype(jnp.float32)
    local_picked = jnp.sum(one_hot * logits, axis=1)
    row_top = lax.pmax(jnp.max(logits, axis=1), "seq")
    shifted = jnp.exp(logits - row_top[:, None])
    row_total, picked = lax.psum((jnp.sum(shifted, axis=1), local_picked), "seq")
    log_total = row_top + jnp.log(row_total)
    probs = shifted / row_total[:, None]
    row_loss = log_total - picked
    loss_value = lax.psum(jnp.sum(mask_float * row_loss), "dp") / num_valid
    dlogits = ((probs - one_hot) * (mask_float / num_valid)[:, None]).astype(jnp.bfloat16)
    shard_rows = lax.all_gather(dlogits, "dp", axis=0, tiled=True)
    grad_slices = jnp.dot(shard_rows, head_weight, preferred_element_type=jnp.float32)
    grad_head = lax.dot_general(
        shard_rows, slices, (((0,), (0,)), ((), ())), preferred_element_type=jnp.float32
    )
    returned = lax.all_to_all(grad_slices, "dp", split_axis=0, concat_axis=1, tiled=True)
    grad_normed = lax.psum(returned, "seq")
    grad_gain = lax.psum(jnp.sum(grad_normed * unit_rows, axis=0), "dp")
    grad_hidden = norm_back(grad_normed, unit_rows, inv_rms, gain).astype(jnp.bfloat16)
    return (loss_value, grad_hidden, grad_gain, grad_head)


def body(hidden, gain, head_weight, targets, loss_mask):
    dl, c, ghid, gg, scal, flag = fused(hidden, gain, head_weight, targets, loss_mask)

    def fast(*args):
        gh, ghid_out, gg_out, loss = finish(dl, c, ghid, gg, scal)
        return loss.reshape(()), ghid_out, gg_out.reshape(D), gh

    return lax.cond(flag[0, 0] > 0, general, fast, hidden, gain, head_weight, targets, loss_mask)


def solution(mesh):
    return jax.shard_map(
        body,
        mesh=mesh,
        in_specs=(P("dp", None), P(), P("seq", "dp"), P("dp"), P("dp")),
        out_specs=(P(), P("dp", None), P(), P("seq", "dp")),
        check_vma=False,
    )
```

```python
import jax
import jax.numpy as jnp
from jax import lax
from jax.experimental import pallas as pl
from jax.experimental.pallas import tpu as pltpu
from jax.sharding import PartitionSpec as P

EPS = 1e-05
MESH = pl.DeviceIdType.MESH
F32 = jnp.float32
BF16 = jnp.bfloat16
NT = (((1,), (1,)), ((), ()))

D = 4096
W = 512
B = 128
V = 2632
VP = 2688
CAP = 640
CH = 21
R = VP // CH
RH, RQ, RP = R // 2, R // 4, R // 8
G = 384
LOW = -1e30

LAG1, LAG2, LAG3, LAG4, LAG5 = 8, 14, 20, 28, 36

NSEM = 0


def sems(n):
    global NSEM
    NSEM += n
    return NSEM - n


H0, M0, HC0 = sems(8), sems(8), sems(8)
S10, S20, S30, G30, G20, G10 = [sems(CH) for _ in range(6)]
T10, T20, T30 = sems(4), sems(8), sems(8)
DC0, DX0, DZ0, DP0, AZ0, AX0, AC0 = sems(1), sems(8), sems(8), sems(8), sems(8), sems(8), sems(16)


def kernel(hid_in, gain, wgt_in, tgt, msk, dlo, C, ghid, gg, scal, flag,
           hid, wgt, GTX, H, META, WP, WT, S, HCT, GCOL, ROWS, L, R1, A1, R2, A2, R3, STAT, ST1, ST2, ST3,
           PR, DN, RC, T1, B1, RX, B2, RZ, MB, RB, ss, rs, ls):
    dp = lax.axis_index("dp")
    seq = lax.axis_index("seq")
    y, xh = dp // 2, dp % 2
    z, xl, co = seq // 4, (seq // 2) % 2, seq % 2
    p1, p2 = (y // 2 + y) % 2, y // 2
    ya, yb = (y + 1 - 2 * (y % 2)) * 2 + xh, (3 - y) * 2 + xh
    xpeer = y * 2 + 1 - xh

    def seq_of(zz, xx, cc):
        return zz * 4 + xx * 2 + cc

    def rcopy(src, dst, sem, dev):
        return pltpu.make_async_remote_copy(
            src_ref=src, dst_ref=dst, send_sem=ss.at[sem], recv_sem=rs.at[sem],
            device_id=dev, device_id_type=MESH)

    def rows_at(start, size):
        return pl.ds(pl.multiple_of(start, 16), size)

    dp_peers = [lax.rem(dp + k, 8) for k in range(1, 8)]
    dp_from = [lax.rem(dp + 8 - k, 8) for k in range(1, 8)]
    z_peers = [lax.rem(z + k, 8) for k in range(1, 8)]
    z_from = [lax.rem(z + 8 - k, 8) for k in range(1, 8)]
    g_me = xl * 2 + co
    g_peers = [lax.rem(g_me + k, 4) for k in range(1, 4)]
    g_from = [lax.rem(g_me + 4 - k, 4) for k in range(1, 4)]
    core_dev = (dp, seq_of(z, xl, 1 - co))
    xlo_dev = (dp, seq_of(z, 1 - xl, co))

    fetch_hid = pltpu.make_async_copy(hid_in, hid, ls.at[0])
    fetch_hid.start()
    fetch_wgt = pltpu.make_async_copy(wgt_in, wgt, ls.at[1])
    fetch_wgt.start()

    barrier = pltpu.get_barrier_semaphore()
    for j in dp_peers:
        pl.semaphore_signal(barrier, inc=1, device_id=(j, seq), device_id_type=MESH)
    for g in g_peers:
        pl.semaphore_signal(barrier, inc=1, device_id=(dp, z * 4 + g), device_id_type=MESH)
    for zz in z_peers:
        pl.semaphore_signal(barrier, inc=1, device_id=(dp, seq_of(zz, xl, co)), device_id_type=MESH)

    fetch_hid.wait()
    total = jnp.zeros((B, 1), F32)
    for j in range(8):
        x = hid[:, j * W:(j + 1) * W].astype(F32)
        total = total + jnp.sum(x * x, axis=1, keepdims=True)
    rinv = lax.rsqrt(total * (1.0 / D) + EPS)
    rinv_t = jnp.transpose(jnp.broadcast_to(rinv, (B, B)))
    META[dp] = jnp.concatenate(
        [rinv_t[0:1, :], msk[...].astype(F32), tgt[...].astype(F32), jnp.zeros((5, B), F32)], axis=0)
    H[dp] = hid[:, pl.ds(pl.multiple_of(dp * W, W), W)]
    pl.semaphore_wait(barrier, 17)

    half = pl.ds(pl.multiple_of(co * 64, 64), 64)
    ohalf = pl.ds(pl.multiple_of((1 - co) * 64, 64), 64)
    hsend = []
    msend = []
    for k in range(1, 8):
        j = dp_peers[k - 1]
        c = rcopy(META.at[dp], META.at[dp], M0 + k, (j, seq))
        c.start()
        msend.append(c)
        c = rcopy(hid.at[half, pl.ds(pl.multiple_of(j * W, W), W)], H.at[dp, half, :], H0 + k, (j, seq))
        c.start()
        hsend.append(c)

    fetch_wgt.wait()
    for i in range(6):
        WP[i * G:(i + 1) * G, :] = wgt[i * G:(i + 1) * G, :]
    WP[6 * G:V - 8, :] = wgt[6 * G:V - 8, :]
    WP[V - 8:V + 8, :] = jnp.concatenate(
        [wgt[V - 8:V, :].astype(F32), jnp.zeros((8, W), F32)], axis=0).astype(BF16)
    WP[V + 8:VP, :] = jnp.zeros((VP - V - 8, W), BF16)
    gain_row = jnp.concatenate([gain[pl.ds(dp * 4 + i, 1), :] for i in range(4)], axis=1)
    GCOL[...] = jnp.transpose(jnp.broadcast_to(gain_row, (B, W)))
    STAT[...] = jnp.concatenate([jnp.full((1, CAP), LOW, F32), jnp.zeros((7, CAP), F32)], axis=0)
    DN[...] = jnp.zeros_like(DN)

    for k in range(1, 8):
        j = dp_from[k - 1]
        rcopy(META.at[j], META.at[j], M0 + k, (dp, seq)).wait_recv()
    metas = [META[j] for j in range(8)]
    m8 = jnp.concatenate([m[1:2, :] for m in metas] + [jnp.zeros((8, B), F32)], axis=0)
    tri = (lax.broadcasted_iota(jnp.int32, (B, B), 0) <= lax.broadcasted_iota(jnp.int32, (B, B), 1)).astype(F32)
    cum = jnp.dot(m8.astype(BF16), tri.astype(BF16), preferred_element_type=F32)
    base = jnp.zeros((1, 1), F32)
    slot = lax.broadcasted_iota(jnp.int32, (CAP, B), 0)
    for j in range(8):
        rank = jnp.where(metas[j][1:2, :] > 0.5, cum[j:j + 1, :] + base - 1.0, -1.0).astype(jnp.int32)
        S[:, j * B:(j + 1) * B] = (slot == rank).astype(F32).astype(BF16)
        base = base + jnp.sum(metas[j][1:2, :], axis=1, keepdims=True)
    count = base
    r_all = jnp.concatenate([m[0:1, :] for m in metas], axis=1)
    v_all = jnp.concatenate([m[1:2, :] for m in metas], axis=1)
    t_all = jnp.concatenate([m[2:3, :] for m in metas], axis=1)
    hi = r_all.astype(BF16).astype(F32)
    mid = (r_all - hi).astype(BF16).astype(F32)
    lo = (r_all - hi) - mid
    ta = jnp.floor(t_all * (1.0 / 4096))
    tb = jnp.floor((t_all - ta * 4096) * (1.0 / 64))
    tc = t_all - ta * 4096 - tb * 64
    mr = jnp.concatenate([hi, mid, lo, v_all, ta, tb, tc, jnp.zeros((9, 8 * B), F32)], axis=0).astype(BF16)
    crow = lax.dot_general(mr, S[...], NT, preferred_element_type=F32)
    mr2 = jnp.concatenate([mr, jnp.zeros((B - 16, 8 * B), BF16)], axis=0)
    ccol = lax.dot_general(S[...], mr2, NT, preferred_element_type=F32)
    valid_row = crow[3:4, :]
    tgt_f = crow[4:5, :] * 4096.0 + crow[5:6, :] * 64.0 + crow[6:7, :] - (seq * V).astype(F32)
    here = jnp.logical_and(valid_row > 0.5, jnp.logical_and(tgt_f > -0.5, tgt_f < V - 0.5))
    tgt_f = jnp.where(here, tgt_f, -1.0)
    rinv_col = ccol[:, 0:1] + ccol[:, 1:2] + ccol[:, 2:3]
    ROWS[...] = jnp.concatenate(
        [crow[0:1, :] + crow[1:2, :] + crow[2:3, :], valid_row / count, tgt_f, valid_row,
         jnp.zeros((4, CAP), F32)], axis=0)

    hc = []
    for k in range(1, 8):
        j = dp_from[k - 1]
        rcopy(H.at[j, half, :], H.at[j, half, :], H0 + k, (dp, seq)).wait_recv()
        c = rcopy(H.at[j, half, :], H.at[j, half, :], HC0 + k, core_dev)
        c.start()
        hc.append(c)
    for k in range(1, 8):
        j = dp_from[k - 1]
        rcopy(H.at[j, ohalf, :], H.at[j, ohalf, :], HC0 + k, core_dev).wait_recv()
    hcomp = jnp.dot(S[...], H[...].reshape(8 * B, W), preferred_element_type=F32)
    C[...] = ((hcomp * rinv_col) * gain_row).astype(BF16)

    def axis(c, s):
        a = (c + s) % 3
        e0, e1, e2 = (2 - a) * (1 - a) // 2, a * (2 - a), a * (a - 1) // 2
        return p1 * e0 + p2 * e1 + xh * e2, (ya * e0 + yb * e1 + xpeer * e2, seq)

    def bits(c):
        return axis(c, 0)[0], axis(c, 1)[0], axis(c, 2)[0]

    def s1(c):
        f, g, h = bits(c)
        return rcopy(L.at[rows_at(c * R + (1 - f) * RH, RH), :], R1.at[c], S10 + c, axis(c, 0)[1])

    def s2(c):
        f, g, h = bits(c)
        return rcopy(A1.at[c, rows_at((1 - g) * RQ, RQ), :], R2.at[c], S20 + c, axis(c, 1)[1])

    def s3(c):
        f, g, h = bits(c)
        return rcopy(A2.at[c, rows_at((1 - h) * RP, RP), :], R3.at[c], S30 + c, axis(c, 2)[1])

    def within(start, size, sem, dev):
        return rcopy(PR.at[rows_at(start, size), :], PR.at[rows_at(start, size), :], sem, dev)

    def g3(c, other=0):
        f, g, h = bits(c)
        h = h + other * (1 - 2 * h)
        return within(c * R + f * RH + g * RQ + h * RP, RP, G30 + c, axis(c, 2)[1])

    def g2(c, other=0):
        f, g, h = bits(c)
        g = g + other * (1 - 2 * g)
        return within(c * R + f * RH + g * RQ, RQ, G20 + c, axis(c, 1)[1])

    def g1(c, other=0):
        f, g, h = bits(c)
        f = f + other * (1 - 2 * f)
        return within(c * R + f * RH, RH, G10 + c, axis(c, 0)[1])

    def gather_steps(k):
        @pl.when(jnp.logical_and(k >= LAG4, k < CH + LAG4))
        def _():
            g3(k - LAG4, 1).wait_recv()
            g2(k - LAG4).start()

        @pl.when(jnp.logical_and(k >= LAG5, k < CH + LAG5))
        def _():
            g2(k - LAG5, 1).wait_recv()
            g1(k - LAG5).start()

    @pl.loop(0, CH + LAG3)
    def _(k):
        @pl.when(k < CH)
        def _():
            rows = rows_at(k * R, R)
            L[rows, :] = lax.dot_general(WP[rows, :], C[...], NT, preferred_element_type=F32).astype(BF16)
            s1(k).start()

        @pl.when(jnp.logical_and(k >= LAG1, k < CH + LAG1))
        def _():
            c = k - LAG1
            f, g, h = bits(c)
            s1(c).wait_recv()
            A1[c] = (L[rows_at(c * R + f * RH, RH), :].astype(F32) + R1[c].astype(F32)).astype(BF16)
            s2(c).start()

        @pl.when(jnp.logical_and(k >= LAG2, k < CH + LAG2))
        def _():
            c = k - LAG2
            f, g, h = bits(c)
            s2(c).wait_recv()
            A2[c] = (A1[c, rows_at(g * RQ, RQ), :].astype(F32) + R2[c].astype(F32)).astype(BF16)
            s3(c).start()

        @pl.when(k >= LAG3)
        def _():
            c = k - LAG3
            f, g, h = bits(c)
            s3(c).wait_recv()
            logits = A2[c, rows_at(h * RP, RP), :].astype(F32) + R3[c].astype(F32)
            first = c * R + f * RH + g * RQ + h * RP
            local = first + lax.broadcasted_iota(jnp.int32, (RP, CAP), 0)
            inside = local < V
            ex = jnp.where(inside, jnp.exp(logits), 0.0)
            PR[rows_at(first, RP), :] = ex.astype(BF16)
            g3(c).start()
            hit = local == ROWS[2:3, :].astype(jnp.int32)
            STAT[0:1, :] = jnp.maximum(
                STAT[0:1, :], jnp.max(jnp.where(inside, logits, LOW), axis=0, keepdims=True))
            STAT[1:2, :] = STAT[1:2, :] + jnp.sum(ex, axis=0, keepdims=True)
            STAT[2:3, :] = STAT[2:3, :] + jnp.sum(ex * logits, axis=0, keepdims=True)
            STAT[3:4, :] = STAT[3:4, :] + jnp.sum(jnp.where(hit, logits, 0.0), axis=0, keepdims=True)

        gather_steps(k)

    def merge(slots, n):
        parts = [slots[i] for i in range(n)]
        top = parts[0][0:1, :]
        sums = parts[0][1:4, :]
        for q in parts[1:]:
            top = jnp.maximum(top, q[0:1, :])
            sums = sums + q[1:4, :]
        return jnp.concatenate([top, sums, jnp.zeros((4, CAP), F32)], axis=0)

    sends = []

    def spread(slots, mine, devs, sem):
        for k, dev in enumerate(devs, 1):
            c = rcopy(slots.at[mine], slots.at[mine], sem + k, dev)
            c.start()
            sends.append(c)

    def collect(slots, froms, sem):
        for k, src in enumerate(froms, 1):
            rcopy(slots.at[src], slots.at[src], sem + k, (dp, seq)).wait_recv()

    last = CH + LAG3
    mids = [last + (LAG5 - LAG3) * i // 3 for i in range(4)]
    ST1[g_me] = STAT[...]
    spread(ST1, g_me, [(dp, z * 4 + g) for g in g_peers], T10)
    HCT[...] = jnp.transpose(hcomp)

    @pl.loop(mids[0], mids[1])
    def _(k):
        gather_steps(k)
    collect(ST1, g_from, T10)
    ST2[z] = merge(ST1, 4)
    spread(ST2, z, [(dp, seq_of(zz, xl, co)) for zz in z_peers], T20)

    @pl.loop(0, VP // G)
    def _(i):
        WT[i] = jnp.transpose(WP[pl.ds(pl.multiple_of(i * G, G), G), :])

    @pl.loop(mids[1], mids[2])
    def _(k):
        gather_steps(k)
    collect(ST2, z_from, T20)
    ST3[dp] = merge(ST2, 8)
    spread(ST3, dp, [(j, seq) for j in dp_peers], T30)

    @pl.loop(mids[2], mids[3])
    def _(k):
        gather_steps(k)
    collect(ST3, dp_from, T30)
    stat = merge(ST3, 8)
    top, ssum, esum, tsum = [stat[i:i + 1, :] for i in range(4)]
    share = ROWS[1:2, :]
    valid = ROWS[3:4, :] > 0.5
    loss = jnp.sum(jnp.where(valid, jnp.log(ssum) - tsum, 0.0), axis=1, keepdims=True) / count
    size = jnp.abs(top)
    peak = (1.0 + size) * jnp.exp(top) / ssum
    odd = jnp.where(jnp.logical_and(valid, jnp.logical_or(size > 40.0, peak > 0.25)), 1.0, 0.0)
    odd = jnp.maximum(jnp.max(odd, axis=1, keepdims=True), jnp.where(count > CAP + 0.5, 1.0, 0.0))
    scal[...] = loss
    flag[...] = odd.astype(jnp.int32)
    ROWS[4:5, :] = share / ssum
    ROWS[5:6, :] = (esum / ssum - tsum) * share * (1.0 / D)

    @pl.loop(0, VP // G)
    def _(i):
        for q in range(CH * G // VP):
            g1(i * (CH * G // VP) + q, 1).wait_recv()
        rows = rows_at(i * G, G)
        local = i * G + lax.broadcasted_iota(jnp.int32, (G, CAP), 0)
        hit = local == ROWS[2:3, :].astype(jnp.int32)
        dl = PR[rows, :].astype(F32) * ROWS[4:5, :] - jnp.where(hit, ROWS[1:2, :], 0.0)
        dlo[rows, :] = dl.astype(BF16)
        DN[...] += jnp.dot(WT[i], dlo[rows, :], preferred_element_type=F32)

    dc = rcopy(DN.at[rows_at((1 - co) * 256, 256), :], RC, DC0, core_dev)
    dc.start()
    dc.wait_recv()
    T1[...] = DN[rows_at(co * 256, 256), :] + RC[...]
    far = (4, 3, 5, 2, 6, 1, 7, 0)
    dx = []
    for n, k in enumerate(far):
        zz = lax.rem(z + k, 8)
        B1[zz] = T1[rows_at((1 - xl) * 128 + zz * 16, 16), :]
        c = rcopy(B1.at[zz], RX.at[zz], DX0 + n, xlo_dev)
        c.start()
        dx.append(c)
    dz = []
    for n, k in enumerate(far):
        zz = lax.rem(z + k, 8)
        dx[n].wait_recv()
        part = T1[rows_at(xl * 128 + zz * 16, 16), :] + RX[zz]
        if k:
            B2[zz] = part
            c = rcopy(B2.at[zz], RZ.at[z], DZ0 + k, (dp, seq_of(zz, xl, co)))
            c.start()
            dz.append(c)
    dn = part
    for k in (1, 7, 2, 6, 3, 5, 4):
        rcopy(RZ.at[z_from[k - 1]], RZ.at[z_from[k - 1]], DZ0 + k, (dp, seq)).wait_recv()
        dn = dn + RZ[z_from[k - 1]]

    off = co * 256 + xl * 128 + z * 16
    rinv_row = ROWS[0:1, :]
    xn = HCT[rows_at(off, 16), :] * rinv_row
    gc = GCOL[rows_at(off, 16), 0:1]
    grow = (rinv_row * (dn * gc - xn * ROWS[5:6, :])).astype(BF16)
    ggc = jnp.sum(dn * xn, axis=1, keepdims=True)
    wide_rows = jnp.dot(grow, S[...], preferred_element_type=F32).astype(BF16)
    ghi = ggc.astype(BF16).astype(F32)
    gmid = (ggc - ghi).astype(BF16).astype(F32)
    glo = (ggc - ghi) - gmid
    lane = lax.broadcasted_iota(jnp.int32, (16, B), 1)
    gparts = jnp.where(lane == 0, ghi, jnp.where(lane == 1, gmid, jnp.where(lane == 2, glo, 0.0))).astype(BF16)
    for j in range(8):
        MB[j, 0:16, :] = wide_rows[:, j * B:(j + 1) * B]
        MB[j, 16:32, :] = gparts
    dpc = []
    for k in range(1, 8):
        c = rcopy(MB.at[dp_peers[k - 1]], RB.at[dp], DP0 + k, (dp_peers[k - 1], seq))
        c.start()
        dpc.append(c)
    RB[dp] = MB[dp]
    for k in range(1, 8):
        rcopy(RB.at[dp_from[k - 1]], RB.at[dp_from[k - 1]], DP0 + k, (dp, seq)).wait_recv()

    mine = co * 16 + xl * 8 + z
    GTX[mine, 0:B, :] = RB[:, 0:16, :].reshape(B, B)
    GTX[mine, B:B + 16, :] = jnp.transpose(RB[:, 16:32, :].reshape(B, B).astype(F32))[0:16, :].astype(BF16)

    def slice_copy(i, sem, dev):
        return rcopy(GTX.at[i], GTX.at[i], sem, dev)

    def forward(i, sem, dev):
        c = slice_copy(i, sem, dev)
        c.start()
        sends.append(c)

    row = lax.broadcasted_iota(jnp.int32, (B, B), 0)
    lane = lax.broadcasted_iota(jnp.int32, (B, B), 1)
    pick = (row == lane // 16).astype(F32)
    diag = row % 16 == lane % 16

    def emit(cc, xx):
        q = cc * 2 + xx
        at = pl.ds(q * 8, 8)
        for j in range(8):
            block = GTX[at, j * 16:(j + 1) * 16, :].reshape(B, B)
            ghid[:, pl.ds(pl.multiple_of(j * W + q * B, B), B)] = jnp.transpose(block)
        parts = GTX[at, B:B + 16, :].astype(F32)
        sums = parts[:, 0, :] + parts[:, 1, :] + parts[:, 2, :]
        cols = jnp.transpose(jnp.concatenate([sums, jnp.zeros((B - 8, B), F32)], axis=0))
        spread = jnp.dot(cols, pick, precision=lax.Precision.HIGHEST, preferred_element_type=F32)
        spread = jnp.sum(jnp.where(diag, spread, 0.0).reshape(8, 16, B), axis=1)
        for j in range(8):
            gg[pl.ds(j * 4 + q, 1), :] = spread[j:j + 1, :]

    near = (1, 7, 2, 6, 3, 5, 4)
    ox, oc = 1 - xl, 1 - co
    for k in (4, 3, 5, 2, 6, 1, 7):
        forward(mine, AZ0 + k, (dp, seq_of(z_peers[k - 1], xl, co)))
    forward(mine, AX0, xlo_dev)
    forward(mine, AC0, core_dev)
    for k in near:
        src = co * 16 + xl * 8 + z_from[k - 1]
        slice_copy(src, AZ0 + k, (dp, seq)).wait_recv()
        forward(src, AX0 + k, xlo_dev)
        forward(src, AC0 + k, core_dev)
    emit(co, xl)
    for k in (0,) + near:
        src = co * 16 + ox * 8 + (z_from[k - 1] if k else z)
        slice_copy(src, AX0 + k, (dp, seq)).wait_recv()
        forward(src, AC0 + 8 + k, core_dev)
    emit(co, ox)
    for k in (0,) + near:
        slice_copy(oc * 16 + xl * 8 + (z_from[k - 1] if k else z), AC0 + k, (dp, seq)).wait_recv()
    emit(oc, xl)
    for k in (0,) + near:
        slice_copy(oc * 16 + ox * 8 + (z_from[k - 1] if k else z), AC0 + 8 + k, (dp, seq)).wait_recv()
    emit(oc, ox)

    for c in hsend + msend + hc + sends + [dc] + dx + dz + dpc:
        c.wait_send()

    @pl.loop(0, CH)
    def _(c):
        s1(c).wait_send()
        s2(c).wait_send()
        s3(c).wait_send()
        g3(c).wait_send()
        g2(c).wait_send()
        g1(c).wait_send()


def fused(hidden, gain, head_weight, targets, loss_mask):
    vm = pl.BlockSpec(memory_space=pltpu.VMEM)
    hbm = pl.BlockSpec(memory_space=pl.ANY)
    scratch = [
        pltpu.VMEM((B, D), BF16),
        pltpu.VMEM((V, W), BF16),
        pltpu.VMEM((32, B + 16, B), BF16),
        pltpu.VMEM((8, B, W), BF16),
        pltpu.VMEM((8, 8, B), F32),
        pltpu.VMEM((VP, W), BF16),
        pltpu.VMEM((VP // G, W, G), BF16),
        pltpu.VMEM((CAP, 8 * B), BF16),
        pltpu.VMEM((W, CAP), F32),
        pltpu.VMEM((W, B), F32),
        pltpu.VMEM((8, CAP), F32),
        pltpu.VMEM((VP, CAP), BF16),
        pltpu.VMEM((CH, RH, CAP), BF16),
        pltpu.VMEM((CH, RH, CAP), BF16),
        pltpu.VMEM((CH, RQ, CAP), BF16),
        pltpu.VMEM((CH, RQ, CAP), BF16),
        pltpu.VMEM((CH, RP, CAP), BF16),
        pltpu.VMEM((8, CAP), F32),
        pltpu.VMEM((4, 8, CAP), F32),
        pltpu.VMEM((8, 8, CAP), F32),
        pltpu.VMEM((8, 8, CAP), F32),
        pltpu.VMEM((VP, CAP), BF16),
        pltpu.VMEM((W, CAP), F32),
        pltpu.VMEM((256, CAP), F32),
        pltpu.VMEM((256, CAP), F32),
        pltpu.VMEM((8, 16, CAP), F32),
        pltpu.VMEM((8, 16, CAP), F32),
        pltpu.VMEM((8, 16, CAP), F32),
        pltpu.VMEM((8, 16, CAP), F32),
        pltpu.VMEM((8, 32, B), BF16),
        pltpu.VMEM((8, 32, B), BF16),
        pltpu.SemaphoreType.DMA((NSEM,)),
        pltpu.SemaphoreType.DMA((NSEM,)),
        pltpu.SemaphoreType.DMA((2,)),
    ]
    return pl.pallas_call(
        kernel,
        out_shape=(
            jax.ShapeDtypeStruct((VP, CAP), BF16),
            jax.ShapeDtypeStruct((CAP, W), BF16),
            jax.ShapeDtypeStruct((B, D), BF16),
            jax.ShapeDtypeStruct((32, B), F32),
            jax.ShapeDtypeStruct((1, 1), F32),
            jax.ShapeDtypeStruct((1, 1), jnp.int32),
        ),
        in_specs=[hbm, vm, hbm, vm, vm],
        out_specs=(vm,) * 6,
        scratch_shapes=scratch,
        compiler_params=pltpu.CompilerParams(
            collective_id=0, has_side_effects=True, vmem_limit_bytes=44 * 1024 * 1024),
        cost_estimate=pl.CostEstimate(flops=6 * V * CAP * W, bytes_accessed=16 * 1024 * 1024, transcendentals=0),
        name="fused",
    )(hidden, gain.reshape(32, B), head_weight, targets.reshape(1, B), loss_mask.reshape(1, B))


STEPS = 8


def finish_kernel(dl, c, ghid, gg, scal, gh, ghid_out, gg_out, loss, fs):
    i = pl.program_id(0)
    n = VP // STEPS
    rows = pltpu.make_async_copy(ghid, ghid_out, fs.at[0])

    @pl.when(i == 0)
    def _():
        rows.start()
        gg_out[...] = gg[...]
        loss[...] = scal[...]

    gh[...] = jnp.dot(dl[pl.ds(pl.multiple_of(i * n, 16), n), :], c[...], preferred_element_type=F32)

    @pl.when(i == STEPS - 1)
    def _():
        rows.wait()


def finish(dl, c, ghid, gg, scal):
    vm = pl.BlockSpec(memory_space=pltpu.VMEM)
    n = VP // STEPS
    return pl.pallas_call(
        finish_kernel,
        grid=(STEPS,),
        out_shape=(
            jax.ShapeDtypeStruct((V, W), F32),
            jax.ShapeDtypeStruct((B, D), BF16),
            jax.ShapeDtypeStruct((32, B), F32),
            jax.ShapeDtypeStruct((1, 1), F32),
        ),
        in_specs=[vm] * 5,
        out_specs=(
            pl.BlockSpec((n, W), lambda i: (i, 0)),
            pl.BlockSpec(memory_space=pltpu.HBM),
            pl.BlockSpec((32, B), lambda i: (0, 0)),
            pl.BlockSpec((1, 1), lambda i: (0, 0)),
        ),
        scratch_shapes=[pltpu.SemaphoreType.DMA((1,))],
        compiler_params=pltpu.CompilerParams(vmem_limit_bytes=40 * 1024 * 1024),
        cost_estimate=pl.CostEstimate(flops=2 * V * CAP * W, bytes_accessed=8 * 1024 * 1024, transcendentals=0),
        name="finish",
    )(dl, c, ghid, gg, scal)


def norm_back(grad_normed, unit_rows, inv_rms, gain):
    grad_unit = grad_normed * gain
    return inv_rms * (
        grad_unit - unit_rows * jnp.mean(grad_unit * unit_rows, axis=-1, keepdims=True)
    )


def spread_all(x, name):
    n = lax.axis_size(name)
    copies = jnp.broadcast_to(x[None], (n,) + x.shape)
    return lax.all_to_all(copies, name, split_axis=0, concat_axis=0, tiled=True)


def scatter_sum(x, name):
    n = lax.axis_size(name)
    parts = lax.all_to_all(x, name, split_axis=0, concat_axis=0, tiled=True)
    return jnp.sum(parts.reshape((n, x.shape[0] // n) + x.shape[1:]), axis=0)


def total(x, name):
    return jnp.sum(spread_all(x, name), axis=0)


def general(hidden, gain, head_weight, targets, loss_mask):
    floats = hidden.astype(jnp.float32)
    inv_rms = lax.rsqrt(jnp.mean(floats * floats, axis=-1, keepdims=True) + EPS)
    unit_rows = floats * inv_rms
    normed = (unit_rows * gain).astype(jnp.bfloat16)
    mask_float = loss_mask.astype(jnp.float32)
    num_valid = total(jnp.sum(mask_float).reshape(1), "dp")[0]
    slices = lax.all_to_all(normed, "dp", split_axis=1, concat_axis=0, tiled=True)
    vocab_rows = head_weight.shape[0]
    logits = scatter_sum(
        lax.dot_general(slices, head_weight, NT, preferred_element_type=jnp.float32), "dp")
    column = lax.axis_index("seq") * vocab_rows + jnp.arange(vocab_rows, dtype=jnp.int32)
    one_hot = (column[None, :] == targets[:, None]).astype(jnp.float32)
    local_picked = jnp.sum(one_hot * logits, axis=1)
    row_top = jnp.max(spread_all(jnp.max(logits, axis=1), "seq"), axis=0)
    shifted = jnp.exp(logits - row_top[:, None])
    row_total, picked = total(jnp.stack([jnp.sum(shifted, axis=1), local_picked]), "seq")
    log_total = row_top + jnp.log(row_total)
    probs = shifted / row_total[:, None]
    row_loss = log_total - picked
    loss_value = total(jnp.sum(mask_float * row_loss).reshape(1), "dp")[0] / num_valid
    dlogits = ((probs - one_hot) * (mask_float / num_valid)[:, None]).astype(jnp.bfloat16)
    shard_rows = spread_all(dlogits, "dp").reshape(-1, vocab_rows)
    grad_slices = jnp.dot(shard_rows, head_weight, preferred_element_type=jnp.float32)
    grad_head = lax.dot_general(
        shard_rows, slices, (((0,), (0,)), ((), ())), preferred_element_type=jnp.float32
    )
    returned = lax.all_to_all(grad_slices, "dp", split_axis=0, concat_axis=1, tiled=True)
    mine = scatter_sum(returned, "seq")
    grad_normed = spread_all(mine, "seq").reshape(returned.shape)
    grad_gain = total(jnp.sum(grad_normed * unit_rows, axis=0), "dp")
    grad_hidden = norm_back(grad_normed, unit_rows, inv_rms, gain).astype(jnp.bfloat16)
    return (loss_value, grad_hidden, grad_gain, grad_head)


def body(hidden, gain, head_weight, targets, loss_mask):
    dl, c, ghid, gg, scal, flag = fused(hidden, gain, head_weight, targets, loss_mask)

    def fast(*args):
        gh, ghid_out, gg_out, loss = finish(dl, c, ghid, gg, scal)
        return loss.reshape(()), ghid_out, gg_out.reshape(D), gh

    return lax.cond(flag[0, 0] > 0, general, fast, hidden, gain, head_weight, targets, loss_mask)


def solution(mesh):
    return jax.shard_map(
        body,
        mesh=mesh,
        in_specs=(P("dp", None), P(), P("seq", "dp"), P("dp"), P("dp")),
        out_specs=(P(), P("dp", None), P(), P("seq", "dp")),
        check_vma=False,
    )
```

```python
import jax
import jax.numpy as jnp
from jax import lax
from jax.experimental import pallas as pl
from jax.experimental.pallas import tpu as pltpu
from jax.sharding import PartitionSpec as P

EPS = 1e-05
MESH = pl.DeviceIdType.MESH
F32 = jnp.float32
BF16 = jnp.bfloat16
NT = (((1,), (1,)), ((), ()))

D = 4096
W = 512
B = 128
V = 2632
VP = 2688
CAP = 640
CH = 21
R = VP // CH
RH, RQ, RP = R // 2, R // 4, R // 8
G = 384
LOW = -1e30

LAG1, LAG2, LAG3, LAG4, LAG5 = 8, 14, 20, 28, 36

NSEM = 0


def sems(n):
    global NSEM
    NSEM += n
    return NSEM - n


H0, M0, HC0 = sems(8), sems(8), sems(8)
S10, S20, S30, G30, G20, G10 = [sems(CH) for _ in range(6)]
T10, T20, T30 = sems(4), sems(8), sems(8)
DC0, DX0, DZ0, DP0, AZ0, AX0, AC0 = sems(2), sems(8), sems(8), sems(8), sems(8), sems(8), sems(16)


def kernel(hid_in, gain, wgt_in, tgt, msk, dlo, C, ghid, gg, scal, flag,
           hid, wgt, GTX, H, META, WP, WT, S, HCT, GCOL, ROWS, L, R1, A1, R2, A2, R3, STAT, ST1, ST2, ST3,
           PR, DN, RC, T1, B1, RX, B2, RZ, MB, RB, ss, rs, ls):
    dp = lax.axis_index("dp")
    seq = lax.axis_index("seq")
    y, xh = dp // 2, dp % 2
    z, xl, co = seq // 4, (seq // 2) % 2, seq % 2
    p1, p2 = (y // 2 + y) % 2, y // 2
    ya, yb = (y + 1 - 2 * (y % 2)) * 2 + xh, (3 - y) * 2 + xh
    xpeer = y * 2 + 1 - xh

    def seq_of(zz, xx, cc):
        return zz * 4 + xx * 2 + cc

    def rcopy(src, dst, sem, dev):
        return pltpu.make_async_remote_copy(
            src_ref=src, dst_ref=dst, send_sem=ss.at[sem], recv_sem=rs.at[sem],
            device_id=dev, device_id_type=MESH)

    def rows_at(start, size):
        return pl.ds(pl.multiple_of(start, 16), size)

    dp_peers = [lax.rem(dp + k, 8) for k in range(1, 8)]
    dp_from = [lax.rem(dp + 8 - k, 8) for k in range(1, 8)]
    z_peers = [lax.rem(z + k, 8) for k in range(1, 8)]
    z_from = [lax.rem(z + 8 - k, 8) for k in range(1, 8)]
    g_me = xl * 2 + co
    g_peers = [lax.rem(g_me + k, 4) for k in range(1, 4)]
    g_from = [lax.rem(g_me + 4 - k, 4) for k in range(1, 4)]
    core_dev = (dp, seq_of(z, xl, 1 - co))
    xlo_dev = (dp, seq_of(z, 1 - xl, co))

    fetch_hid = pltpu.make_async_copy(hid_in, hid, ls.at[0])
    fetch_hid.start()
    fetch_wgt = pltpu.make_async_copy(wgt_in, wgt, ls.at[1])
    fetch_wgt.start()

    barrier = pltpu.get_barrier_semaphore()
    for j in dp_peers:
        pl.semaphore_signal(barrier, inc=1, device_id=(j, seq), device_id_type=MESH)
    for g in g_peers:
        pl.semaphore_signal(barrier, inc=1, device_id=(dp, z * 4 + g), device_id_type=MESH)
    for zz in z_peers:
        pl.semaphore_signal(barrier, inc=1, device_id=(dp, seq_of(zz, xl, co)), device_id_type=MESH)

    fetch_hid.wait()
    total = jnp.zeros((B, 1), F32)
    for j in range(8):
        x = hid[:, j * W:(j + 1) * W].astype(F32)
        total = total + jnp.sum(x * x, axis=1, keepdims=True)
    rinv = lax.rsqrt(total * (1.0 / D) + EPS)
    rinv_t = jnp.transpose(jnp.broadcast_to(rinv, (B, B)))
    META[dp] = jnp.concatenate(
        [rinv_t[0:1, :], msk[...].astype(F32), tgt[...].astype(F32), jnp.zeros((5, B), F32)], axis=0)
    H[dp] = hid[:, pl.ds(pl.multiple_of(dp * W, W), W)]
    pl.semaphore_wait(barrier, 17)

    half = pl.ds(pl.multiple_of(co * 64, 64), 64)
    ohalf = pl.ds(pl.multiple_of((1 - co) * 64, 64), 64)
    hsend = []
    msend = []
    for k in range(1, 8):
        j = dp_peers[k - 1]
        c = rcopy(META.at[dp], META.at[dp], M0 + k, (j, seq))
        c.start()
        msend.append(c)
        c = rcopy(hid.at[half, pl.ds(pl.multiple_of(j * W, W), W)], H.at[dp, half, :], H0 + k, (j, seq))
        c.start()
        hsend.append(c)

    fetch_wgt.wait()
    for i in range(6):
        WP[i * G:(i + 1) * G, :] = wgt[i * G:(i + 1) * G, :]
    WP[6 * G:V - 8, :] = wgt[6 * G:V - 8, :]
    WP[V - 8:V + 8, :] = jnp.concatenate(
        [wgt[V - 8:V, :].astype(F32), jnp.zeros((8, W), F32)], axis=0).astype(BF16)
    WP[V + 8:VP, :] = jnp.zeros((VP - V - 8, W), BF16)
    gain_row = jnp.concatenate([gain[pl.ds(dp * 4 + i, 1), :] for i in range(4)], axis=1)
    GCOL[...] = jnp.transpose(jnp.broadcast_to(gain_row, (B, W)))
    STAT[...] = jnp.concatenate([jnp.full((1, CAP), LOW, F32), jnp.zeros((7, CAP), F32)], axis=0)
    DN[...] = jnp.zeros_like(DN)

    for k in range(1, 8):
        j = dp_from[k - 1]
        rcopy(META.at[j], META.at[j], M0 + k, (dp, seq)).wait_recv()
    metas = [META[j] for j in range(8)]
    m8 = jnp.concatenate([m[1:2, :] for m in metas] + [jnp.zeros((8, B), F32)], axis=0)
    tri = (lax.broadcasted_iota(jnp.int32, (B, B), 0) <= lax.broadcasted_iota(jnp.int32, (B, B), 1)).astype(F32)
    cum = jnp.dot(m8.astype(BF16), tri.astype(BF16), preferred_element_type=F32)
    base = jnp.zeros((1, 1), F32)
    slot = lax.broadcasted_iota(jnp.int32, (CAP, B), 0)
    for j in range(8):
        rank = jnp.where(metas[j][1:2, :] > 0.5, cum[j:j + 1, :] + base - 1.0, -1.0).astype(jnp.int32)
        S[:, j * B:(j + 1) * B] = (slot == rank).astype(F32).astype(BF16)
        base = base + jnp.sum(metas[j][1:2, :], axis=1, keepdims=True)
    count = base
    r_all = jnp.concatenate([m[0:1, :] for m in metas], axis=1)
    v_all = jnp.concatenate([m[1:2, :] for m in metas], axis=1)
    t_all = jnp.concatenate([m[2:3, :] for m in metas], axis=1)
    hi = r_all.astype(BF16).astype(F32)
    mid = (r_all - hi).astype(BF16).astype(F32)
    lo = (r_all - hi) - mid
    ta = jnp.floor(t_all * (1.0 / 4096))
    tb = jnp.floor((t_all - ta * 4096) * (1.0 / 64))
    tc = t_all - ta * 4096 - tb * 64
    mr = jnp.concatenate([hi, mid, lo, v_all, ta, tb, tc, jnp.zeros((9, 8 * B), F32)], axis=0).astype(BF16)
    crow = lax.dot_general(mr, S[...], NT, preferred_element_type=F32)
    mr2 = jnp.concatenate([mr, jnp.zeros((B - 16, 8 * B), BF16)], axis=0)
    ccol = lax.dot_general(S[...], mr2, NT, preferred_element_type=F32)
    valid_row = crow[3:4, :]
    tgt_f = crow[4:5, :] * 4096.0 + crow[5:6, :] * 64.0 + crow[6:7, :] - (seq * V).astype(F32)
    here = jnp.logical_and(valid_row > 0.5, jnp.logical_and(tgt_f > -0.5, tgt_f < V - 0.5))
    tgt_f = jnp.where(here, tgt_f, -1.0)
    rinv_col = ccol[:, 0:1] + ccol[:, 1:2] + ccol[:, 2:3]
    ROWS[...] = jnp.concatenate(
        [crow[0:1, :] + crow[1:2, :] + crow[2:3, :], valid_row / count, tgt_f, valid_row,
         jnp.zeros((4, CAP), F32)], axis=0)

    hc = []
    for k in range(1, 8):
        j = dp_from[k - 1]
        rcopy(H.at[j, half, :], H.at[j, half, :], H0 + k, (dp, seq)).wait_recv()
        c = rcopy(H.at[j, half, :], H.at[j, half, :], HC0 + k, core_dev)
        c.start()
        hc.append(c)
    for k in range(1, 8):
        j = dp_from[k - 1]
        rcopy(H.at[j, ohalf, :], H.at[j, ohalf, :], HC0 + k, core_dev).wait_recv()
    hcomp = jnp.dot(S[...], H[...].reshape(8 * B, W), preferred_element_type=F32)
    C[...] = ((hcomp * rinv_col) * gain_row).astype(BF16)

    def axis(c, s):
        a = (c + s) % 3
        e0, e1, e2 = (2 - a) * (1 - a) // 2, a * (2 - a), a * (a - 1) // 2
        return p1 * e0 + p2 * e1 + xh * e2, (ya * e0 + yb * e1 + xpeer * e2, seq)

    def bits(c):
        return axis(c, 0)[0], axis(c, 1)[0], axis(c, 2)[0]

    def s1(c):
        f, g, h = bits(c)
        return rcopy(L.at[rows_at(c * R + (1 - f) * RH, RH), :], R1.at[c], S10 + c, axis(c, 0)[1])

    def s2(c):
        f, g, h = bits(c)
        return rcopy(A1.at[c, rows_at((1 - g) * RQ, RQ), :], R2.at[c], S20 + c, axis(c, 1)[1])

    def s3(c):
        f, g, h = bits(c)
        return rcopy(A2.at[c, rows_at((1 - h) * RP, RP), :], R3.at[c], S30 + c, axis(c, 2)[1])

    def within(start, size, sem, dev):
        return rcopy(PR.at[rows_at(start, size), :], PR.at[rows_at(start, size), :], sem, dev)

    def g3(c, other=0):
        f, g, h = bits(c)
        h = h + other * (1 - 2 * h)
        return within(c * R + f * RH + g * RQ + h * RP, RP, G30 + c, axis(c, 2)[1])

    def g2(c, other=0):
        f, g, h = bits(c)
        g = g + other * (1 - 2 * g)
        return within(c * R + f * RH + g * RQ, RQ, G20 + c, axis(c, 1)[1])

    def g1(c, other=0):
        f, g, h = bits(c)
        f = f + other * (1 - 2 * f)
        return within(c * R + f * RH, RH, G10 + c, axis(c, 0)[1])

    def gather_steps(k):
        @pl.when(jnp.logical_and(k >= LAG4, k < CH + LAG4))
        def _():
            g3(k - LAG4, 1).wait_recv()
            g2(k - LAG4).start()

        @pl.when(jnp.logical_and(k >= LAG5, k < CH + LAG5))
        def _():
            g2(k - LAG5, 1).wait_recv()
            g1(k - LAG5).start()

    @pl.loop(0, CH + LAG3)
    def _(k):
        @pl.when(k < CH)
        def _():
            rows = rows_at(k * R, R)
            L[rows, :] = lax.dot_general(WP[rows, :], C[...], NT, preferred_element_type=F32).astype(BF16)
            s1(k).start()

        @pl.when(jnp.logical_and(k >= LAG1, k < CH + LAG1))
        def _():
            c = k - LAG1
            f, g, h = bits(c)
            s1(c).wait_recv()
            A1[c] = (L[rows_at(c * R + f * RH, RH), :].astype(F32) + R1[c].astype(F32)).astype(BF16)
            s2(c).start()

        @pl.when(jnp.logical_and(k >= LAG2, k < CH + LAG2))
        def _():
            c = k - LAG2
            f, g, h = bits(c)
            s2(c).wait_recv()
            A2[c] = (A1[c, rows_at(g * RQ, RQ), :].astype(F32) + R2[c].astype(F32)).astype(BF16)
            s3(c).start()

        @pl.when(k >= LAG3)
        def _():
            c = k - LAG3
            f, g, h = bits(c)
            s3(c).wait_recv()
            logits = A2[c, rows_at(h * RP, RP), :].astype(F32) + R3[c].astype(F32)
            first = c * R + f * RH + g * RQ + h * RP
            local = first + lax.broadcasted_iota(jnp.int32, (RP, CAP), 0)
            inside = local < V
            ex = jnp.where(inside, jnp.exp(logits), 0.0)
            PR[rows_at(first, RP), :] = ex.astype(BF16)
            g3(c).start()
            hit = local == ROWS[2:3, :].astype(jnp.int32)
            STAT[0:1, :] = jnp.maximum(
                STAT[0:1, :], jnp.max(jnp.where(inside, logits, LOW), axis=0, keepdims=True))
            STAT[1:2, :] = STAT[1:2, :] + jnp.sum(ex, axis=0, keepdims=True)
            STAT[2:3, :] = STAT[2:3, :] + jnp.sum(ex * logits, axis=0, keepdims=True)
            STAT[3:4, :] = STAT[3:4, :] + jnp.sum(jnp.where(hit, logits, 0.0), axis=0, keepdims=True)

        gather_steps(k)

    def merge(slots, n):
        parts = [slots[i] for i in range(n)]
        top = parts[0][0:1, :]
        sums = parts[0][1:4, :]
        for q in parts[1:]:
            top = jnp.maximum(top, q[0:1, :])
            sums = sums + q[1:4, :]
        return jnp.concatenate([top, sums, jnp.zeros((4, CAP), F32)], axis=0)

    sends = []

    def spread(slots, mine, devs, sem):
        for k, dev in enumerate(devs, 1):
            c = rcopy(slots.at[mine], slots.at[mine], sem + k, dev)
            c.start()
            sends.append(c)

    def collect(slots, froms, sem):
        for k, src in enumerate(froms, 1):
            rcopy(slots.at[src], slots.at[src], sem + k, (dp, seq)).wait_recv()

    last = CH + LAG3
    mids = [last + (LAG5 - LAG3) * i // 3 for i in range(4)]
    ST1[g_me] = STAT[...]
    spread(ST1, g_me, [(dp, z * 4 + g) for g in g_peers], T10)
    HCT[...] = jnp.transpose(hcomp)

    @pl.loop(mids[0], mids[1])
    def _(k):
        gather_steps(k)
    collect(ST1, g_from, T10)
    ST2[z] = merge(ST1, 4)
    spread(ST2, z, [(dp, seq_of(zz, xl, co)) for zz in z_peers], T20)

    @pl.loop(0, VP // G)
    def _(i):
        WT[i] = jnp.transpose(WP[pl.ds(pl.multiple_of(i * G, G), G), :])

    @pl.loop(mids[1], mids[2])
    def _(k):
        gather_steps(k)
    collect(ST2, z_from, T20)
    ST3[dp] = merge(ST2, 8)
    spread(ST3, dp, [(j, seq) for j in dp_peers], T30)

    @pl.loop(mids[2], mids[3])
    def _(k):
        gather_steps(k)
    collect(ST3, dp_from, T30)
    stat = merge(ST3, 8)
    top, ssum, esum, tsum = [stat[i:i + 1, :] for i in range(4)]
    share = ROWS[1:2, :]
    valid = ROWS[3:4, :] > 0.5
    loss = jnp.sum(jnp.where(valid, jnp.log(ssum) - tsum, 0.0), axis=1, keepdims=True) / count
    size = jnp.abs(top)
    peak = (1.0 + size) * jnp.exp(top) / ssum
    odd = jnp.where(jnp.logical_and(valid, jnp.logical_or(size > 40.0, peak > 0.25)), 1.0, 0.0)
    odd = jnp.maximum(jnp.max(odd, axis=1, keepdims=True), jnp.where(count > CAP + 0.5, 1.0, 0.0))
    scal[...] = loss
    flag[...] = odd.astype(jnp.int32)
    ROWS[4:5, :] = share / ssum
    ROWS[5:6, :] = (esum / ssum - tsum) * share * (1.0 / D)

    @pl.loop(0, VP // G)
    def _(i):
        for q in range(CH * G // VP):
            g1(i * (CH * G // VP) + q, 1).wait_recv()
        rows = rows_at(i * G, G)
        local = i * G + lax.broadcasted_iota(jnp.int32, (G, CAP), 0)
        hit = local == ROWS[2:3, :].astype(jnp.int32)
        dl = PR[rows, :].astype(F32) * ROWS[4:5, :] - jnp.where(hit, ROWS[1:2, :], 0.0)
        dlo[rows, :] = dl.astype(BF16)
        DN[...] += jnp.dot(WT[i], dlo[rows, :], preferred_element_type=F32)

    pass_on, keep = (1 - xl) * 128, xl * 128
    dc = []
    for n, start in enumerate((pass_on, keep)):
        c = rcopy(DN.at[rows_at((1 - co) * 256 + start, 128), :], RC.at[rows_at(start, 128), :], DC0 + n, core_dev)
        c.start()
        dc.append(c)
    dc[0].wait_recv()
    far = (4, 3, 5, 2, 6, 1, 7, 0)
    dx = []
    for n, k in enumerate(far):
        zz = lax.rem(z + k, 8)
        at = pass_on + zz * 16
        B1[zz] = DN[rows_at(co * 256 + at, 16), :] + RC[rows_at(at, 16), :]
        c = rcopy(B1.at[zz], RX.at[zz], DX0 + n, xlo_dev)
        c.start()
        dx.append(c)
    dc[1].wait_recv()
    T1[...] = DN[rows_at(co * 256 + keep, 128), :] + RC[rows_at(keep, 128), :]
    dz = []
    for n, k in enumerate(far):
        zz = lax.rem(z + k, 8)
        dx[n].wait_recv()
        part = T1[rows_at(zz * 16, 16), :] + RX[zz]
        if k:
            B2[zz] = part
            c = rcopy(B2.at[zz], RZ.at[z], DZ0 + k, (dp, seq_of(zz, xl, co)))
            c.start()
            dz.append(c)
    dn = part
    for k in (1, 7, 2, 6, 3, 5, 4):
        rcopy(RZ.at[z_from[k - 1]], RZ.at[z_from[k - 1]], DZ0 + k, (dp, seq)).wait_recv()
        dn = dn + RZ[z_from[k - 1]]

    off = co * 256 + xl * 128 + z * 16
    rinv_row = ROWS[0:1, :]
    xn = HCT[rows_at(off, 16), :] * rinv_row
    gc = GCOL[rows_at(off, 16), 0:1]
    grow = (rinv_row * (dn * gc - xn * ROWS[5:6, :])).astype(BF16)
    ggc = jnp.sum(dn * xn, axis=1, keepdims=True)
    wide_rows = jnp.dot(grow, S[...], preferred_element_type=F32).astype(BF16)
    ghi = ggc.astype(BF16).astype(F32)
    gmid = (ggc - ghi).astype(BF16).astype(F32)
    glo = (ggc - ghi) - gmid
    lane = lax.broadcasted_iota(jnp.int32, (16, B), 1)
    gparts = jnp.where(lane == 0, ghi, jnp.where(lane == 1, gmid, jnp.where(lane == 2, glo, 0.0))).astype(BF16)
    for j in range(8):
        MB[j, 0:16, :] = wide_rows[:, j * B:(j + 1) * B]
        MB[j, 16:32, :] = gparts
    dpc = []
    for k in range(1, 8):
        c = rcopy(MB.at[dp_peers[k - 1]], RB.at[dp], DP0 + k, (dp_peers[k - 1], seq))
        c.start()
        dpc.append(c)
    RB[dp] = MB[dp]
    for k in range(1, 8):
        rcopy(RB.at[dp_from[k - 1]], RB.at[dp_from[k - 1]], DP0 + k, (dp, seq)).wait_recv()

    mine = co * 16 + xl * 8 + z
    GTX[mine, 0:B, :] = RB[:, 0:16, :].reshape(B, B)
    GTX[mine, B:B + 16, :] = jnp.transpose(RB[:, 16:32, :].reshape(B, B).astype(F32))[0:16, :].astype(BF16)

    def slice_copy(i, sem, dev):
        return rcopy(GTX.at[i], GTX.at[i], sem, dev)

    def forward(i, sem, dev):
        c = slice_copy(i, sem, dev)
        c.start()
        sends.append(c)

    row = lax.broadcasted_iota(jnp.int32, (B, B), 0)
    lane = lax.broadcasted_iota(jnp.int32, (B, B), 1)
    pick = (row == lane // 16).astype(F32)
    diag = row % 16 == lane % 16

    def emit(cc, xx):
        q = cc * 2 + xx
        at = pl.ds(q * 8, 8)
        for j in range(8):
            block = GTX[at, j * 16:(j + 1) * 16, :].reshape(B, B)
            ghid[:, pl.ds(pl.multiple_of(j * W + q * B, B), B)] = jnp.transpose(block)
        parts = GTX[at, B:B + 16, :].astype(F32)
        sums = parts[:, 0, :] + parts[:, 1, :] + parts[:, 2, :]
        cols = jnp.transpose(jnp.concatenate([sums, jnp.zeros((B - 8, B), F32)], axis=0))
        spread = jnp.dot(cols, pick, precision=lax.Precision.HIGHEST, preferred_element_type=F32)
        spread = jnp.sum(jnp.where(diag, spread, 0.0).reshape(8, 16, B), axis=1)
        for j in range(8):
            gg[pl.ds(j * 4 + q, 1), :] = spread[j:j + 1, :]

    near = (1, 7, 2, 6, 3, 5, 4)
    ox, oc = 1 - xl, 1 - co
    for k in (4, 3, 5, 2, 6, 1, 7):
        forward(mine, AZ0 + k, (dp, seq_of(z_peers[k - 1], xl, co)))
    forward(mine, AX0, xlo_dev)
    forward(mine, AC0, core_dev)
    for k in near:
        src = co * 16 + xl * 8 + z_from[k - 1]
        slice_copy(src, AZ0 + k, (dp, seq)).wait_recv()
        forward(src, AX0 + k, xlo_dev)
        forward(src, AC0 + k, core_dev)
    emit(co, xl)
    for k in (0,) + near:
        src = co * 16 + ox * 8 + (z_from[k - 1] if k else z)
        slice_copy(src, AX0 + k, (dp, seq)).wait_recv()
        forward(src, AC0 + 8 + k, core_dev)
    emit(co, ox)
    for k in (0,) + near:
        slice_copy(oc * 16 + xl * 8 + (z_from[k - 1] if k else z), AC0 + k, (dp, seq)).wait_recv()
    emit(oc, xl)
    for k in (0,) + near:
        slice_copy(oc * 16 + ox * 8 + (z_from[k - 1] if k else z), AC0 + 8 + k, (dp, seq)).wait_recv()
    emit(oc, ox)

    for c in hsend + msend + hc + sends + dc + dx + dz + dpc:
        c.wait_send()

    @pl.loop(0, CH)
    def _(c):
        s1(c).wait_send()
        s2(c).wait_send()
        s3(c).wait_send()
        g3(c).wait_send()
        g2(c).wait_send()
        g1(c).wait_send()


def fused(hidden, gain, head_weight, targets, loss_mask):
    vm = pl.BlockSpec(memory_space=pltpu.VMEM)
    hbm = pl.BlockSpec(memory_space=pl.ANY)
    scratch = [
        pltpu.VMEM((B, D), BF16),
        pltpu.VMEM((V, W), BF16),
        pltpu.VMEM((32, B + 16, B), BF16),
        pltpu.VMEM((8, B, W), BF16),
        pltpu.VMEM((8, 8, B), F32),
        pltpu.VMEM((VP, W), BF16),
        pltpu.VMEM((VP // G, W, G), BF16),
        pltpu.VMEM((CAP, 8 * B), BF16),
        pltpu.VMEM((W, CAP), F32),
        pltpu.VMEM((W, B), F32),
        pltpu.VMEM((8, CAP), F32),
        pltpu.VMEM((VP, CAP), BF16),
        pltpu.VMEM((CH, RH, CAP), BF16),
        pltpu.VMEM((CH, RH, CAP), BF16),
        pltpu.VMEM((CH, RQ, CAP), BF16),
        pltpu.VMEM((CH, RQ, CAP), BF16),
        pltpu.VMEM((CH, RP, CAP), BF16),
        pltpu.VMEM((8, CAP), F32),
        pltpu.VMEM((4, 8, CAP), F32),
        pltpu.VMEM((8, 8, CAP), F32),
        pltpu.VMEM((8, 8, CAP), F32),
        pltpu.VMEM((VP, CAP), BF16),
        pltpu.VMEM((W, CAP), F32),
        pltpu.VMEM((256, CAP), F32),
        pltpu.VMEM((128, CAP), F32),
        pltpu.VMEM((8, 16, CAP), F32),
        pltpu.VMEM((8, 16, CAP), F32),
        pltpu.VMEM((8, 16, CAP), F32),
        pltpu.VMEM((8, 16, CAP), F32),
        pltpu.VMEM((8, 32, B), BF16),
        pltpu.VMEM((8, 32, B), BF16),
        pltpu.SemaphoreType.DMA((NSEM,)),
        pltpu.SemaphoreType.DMA((NSEM,)),
        pltpu.SemaphoreType.DMA((2,)),
    ]
    return pl.pallas_call(
        kernel,
        out_shape=(
            jax.ShapeDtypeStruct((VP, CAP), BF16),
            jax.ShapeDtypeStruct((CAP, W), BF16),
            jax.ShapeDtypeStruct((B, D), BF16),
            jax.ShapeDtypeStruct((32, B), F32),
            jax.ShapeDtypeStruct((1, 1), F32),
            jax.ShapeDtypeStruct((1, 1), jnp.int32),
        ),
        in_specs=[hbm, vm, hbm, vm, vm],
        out_specs=(vm,) * 6,
        scratch_shapes=scratch,
        compiler_params=pltpu.CompilerParams(
            collective_id=0, has_side_effects=True, vmem_limit_bytes=44 * 1024 * 1024),
        cost_estimate=pl.CostEstimate(flops=6 * V * CAP * W, bytes_accessed=16 * 1024 * 1024, transcendentals=0),
        name="fused",
    )(hidden, gain.reshape(32, B), head_weight, targets.reshape(1, B), loss_mask.reshape(1, B))


STEPS = 4


def finish_kernel(dl, c, ghid, gg, scal, gh, ghid_out, gg_out, loss, fs):
    i = pl.program_id(0)
    n = VP // STEPS
    rows = pltpu.make_async_copy(ghid, ghid_out, fs.at[0])

    @pl.when(i == 0)
    def _():
        rows.start()
        gg_out[...] = gg[...]
        loss[...] = scal[...]

    gh[...] = jnp.dot(dl[pl.ds(pl.multiple_of(i * n, 16), n), :], c[...], preferred_element_type=F32)

    @pl.when(i == STEPS - 1)
    def _():
        rows.wait()


def finish(dl, c, ghid, gg, scal):
    vm = pl.BlockSpec(memory_space=pltpu.VMEM)
    n = VP // STEPS
    return pl.pallas_call(
        finish_kernel,
        grid=(STEPS,),
        out_shape=(
            jax.ShapeDtypeStruct((V, W), F32),
            jax.ShapeDtypeStruct((B, D), BF16),
            jax.ShapeDtypeStruct((32, B), F32),
            jax.ShapeDtypeStruct((1, 1), F32),
        ),
        in_specs=[vm] * 5,
        out_specs=(
            pl.BlockSpec((n, W), lambda i: (i, 0)),
            pl.BlockSpec(memory_space=pltpu.HBM),
            pl.BlockSpec((32, B), lambda i: (0, 0)),
            pl.BlockSpec((1, 1), lambda i: (0, 0)),
        ),
        scratch_shapes=[pltpu.SemaphoreType.DMA((1,))],
        compiler_params=pltpu.CompilerParams(vmem_limit_bytes=40 * 1024 * 1024),
        cost_estimate=pl.CostEstimate(flops=2 * V * CAP * W, bytes_accessed=8 * 1024 * 1024, transcendentals=0),
        name="finish",
    )(dl, c, ghid, gg, scal)


def norm_back(grad_normed, unit_rows, inv_rms, gain):
    grad_unit = grad_normed * gain
    return inv_rms * (
        grad_unit - unit_rows * jnp.mean(grad_unit * unit_rows, axis=-1, keepdims=True)
    )


def spread_all(x, name):
    n = lax.axis_size(name)
    copies = jnp.broadcast_to(x[None], (n,) + x.shape)
    return lax.all_to_all(copies, name, split_axis=0, concat_axis=0, tiled=True)


def scatter_sum(x, name):
    n = lax.axis_size(name)
    parts = lax.all_to_all(x, name, split_axis=0, concat_axis=0, tiled=True)
    return jnp.sum(parts.reshape((n, x.shape[0] // n) + x.shape[1:]), axis=0)


def total(x, name):
    return jnp.sum(spread_all(x, name), axis=0)


def general(hidden, gain, head_weight, targets, loss_mask):
    floats = hidden.astype(jnp.float32)
    inv_rms = lax.rsqrt(jnp.mean(floats * floats, axis=-1, keepdims=True) + EPS)
    unit_rows = floats * inv_rms
    normed = (unit_rows * gain).astype(jnp.bfloat16)
    mask_float = loss_mask.astype(jnp.float32)
    num_valid = total(jnp.sum(mask_float).reshape(1), "dp")[0]
    slices = lax.all_to_all(normed, "dp", split_axis=1, concat_axis=0, tiled=True)
    vocab_rows = head_weight.shape[0]
    logits = scatter_sum(
        lax.dot_general(slices, head_weight, NT, preferred_element_type=jnp.float32), "dp")
    column = lax.axis_index("seq") * vocab_rows + jnp.arange(vocab_rows, dtype=jnp.int32)
    one_hot = (column[None, :] == targets[:, None]).astype(jnp.float32)
    local_picked = jnp.sum(one_hot * logits, axis=1)
    row_top = jnp.max(spread_all(jnp.max(logits, axis=1), "seq"), axis=0)
    shifted = jnp.exp(logits - row_top[:, None])
    row_total, picked = total(jnp.stack([jnp.sum(shifted, axis=1), local_picked]), "seq")
    log_total = row_top + jnp.log(row_total)
    probs = shifted / row_total[:, None]
    row_loss = log_total - picked
    loss_value = total(jnp.sum(mask_float * row_loss).reshape(1), "dp")[0] / num_valid
    dlogits = ((probs - one_hot) * (mask_float / num_valid)[:, None]).astype(jnp.bfloat16)
    shard_rows = spread_all(dlogits, "dp").reshape(-1, vocab_rows)
    grad_slices = jnp.dot(shard_rows, head_weight, preferred_element_type=jnp.float32)
    grad_head = lax.dot_general(
        shard_rows, slices, (((0,), (0,)), ((), ())), preferred_element_type=jnp.float32
    )
    returned = lax.all_to_all(grad_slices, "dp", split_axis=0, concat_axis=1, tiled=True)
    mine = scatter_sum(returned, "seq")
    grad_normed = spread_all(mine, "seq").reshape(returned.shape)
    grad_gain = total(jnp.sum(grad_normed * unit_rows, axis=0), "dp")
    grad_hidden = norm_back(grad_normed, unit_rows, inv_rms, gain).astype(jnp.bfloat16)
    return (loss_value, grad_hidden, grad_gain, grad_head)


def body(hidden, gain, head_weight, targets, loss_mask):
    dl, c, ghid, gg, scal, flag = fused(hidden, gain, head_weight, targets, loss_mask)

    def fast(*args):
        gh, ghid_out, gg_out, loss = finish(dl, c, ghid, gg, scal)
        return loss.reshape(()), ghid_out, gg_out.reshape(D), gh

    return lax.cond(flag[0, 0] > 0, general, fast, hidden, gain, head_weight, targets, loss_mask)


def solution(mesh):
    return jax.shard_map(
        body,
        mesh=mesh,
        in_specs=(P("dp", None), P(), P("seq", "dp"), P("dp"), P("dp")),
        out_specs=(P(), P("dp", None), P(), P("seq", "dp")),
        check_vma=False,
    )
```

```python
import jax
import jax.numpy as jnp
from jax import lax
from jax.experimental import pallas as pl
from jax.experimental.pallas import tpu as pltpu
from jax.sharding import PartitionSpec as P

EPS = 1e-05
MESH = pl.DeviceIdType.MESH
F32 = jnp.float32
BF16 = jnp.bfloat16
NT = (((1,), (1,)), ((), ()))

D = 4096
W = 512
B = 128
V = 2632
VP = 2688
CAP = 640
CH = 21
R = VP // CH
RH, RQ, RP = R // 2, R // 4, R // 8
G = 384
LOW = -1e30

LAG1, LAG2, LAG3, LAG4, LAG5 = 8, 14, 20, 28, 36

NSEM = 0


def sems(n):
    global NSEM
    NSEM += n
    return NSEM - n


H0, M0, HC0 = sems(8), sems(8), sems(8)
S10, S20, S30, G30, G20, G10 = [sems(CH) for _ in range(6)]
T10, T20, T30 = sems(4), sems(8), sems(8)
DC0, DX0, DZ0, DP0, AZ0, AX0, AC0 = sems(2), sems(8), sems(8), sems(8), sems(8), sems(8), sems(16)


def kernel(hid_in, gain, wgt_in, tgt, msk, dlo, C, ghid, gg, scal, flag,
           hid, wgt, GTX, H, META, WP, WT, S, HCT, GCOL, ROWS, L, R1, A1, R2, A2, R3, STAT, ST1, ST2, ST3,
           PR, DN, RC, T1, B1, RX, B2, RZ, MB, RB, ss, rs, ls):
    dp = lax.axis_index("dp")
    seq = lax.axis_index("seq")
    y, xh = dp // 2, dp % 2
    z, xl, co = seq // 4, (seq // 2) % 2, seq % 2
    p1, p2 = (y // 2 + y) % 2, y // 2
    ya, yb = (y + 1 - 2 * (y % 2)) * 2 + xh, (3 - y) * 2 + xh
    xpeer = y * 2 + 1 - xh

    def seq_of(zz, xx, cc):
        return zz * 4 + xx * 2 + cc

    def rcopy(src, dst, sem, dev):
        return pltpu.make_async_remote_copy(
            src_ref=src, dst_ref=dst, send_sem=ss.at[sem], recv_sem=rs.at[sem],
            device_id=dev, device_id_type=MESH)

    def rows_at(start, size):
        return pl.ds(pl.multiple_of(start, 16), size)

    dp_peers = [lax.rem(dp + k, 8) for k in range(1, 8)]
    dp_from = [lax.rem(dp + 8 - k, 8) for k in range(1, 8)]
    z_peers = [lax.rem(z + k, 8) for k in range(1, 8)]
    z_from = [lax.rem(z + 8 - k, 8) for k in range(1, 8)]
    g_me = xl * 2 + co
    g_peers = [lax.rem(g_me + k, 4) for k in range(1, 4)]
    g_from = [lax.rem(g_me + 4 - k, 4) for k in range(1, 4)]
    core_dev = (dp, seq_of(z, xl, 1 - co))
    xlo_dev = (dp, seq_of(z, 1 - xl, co))

    fetch_hid = pltpu.make_async_copy(hid_in, hid, ls.at[0])
    fetch_hid.start()

    barrier = pltpu.get_barrier_semaphore()
    for j in dp_peers:
        pl.semaphore_signal(barrier, inc=1, device_id=(j, seq), device_id_type=MESH)
    for g in g_peers:
        pl.semaphore_signal(barrier, inc=1, device_id=(dp, z * 4 + g), device_id_type=MESH)
    for zz in z_peers:
        pl.semaphore_signal(barrier, inc=1, device_id=(dp, seq_of(zz, xl, co)), device_id_type=MESH)

    fetch_hid.wait()
    fetch_wgt = pltpu.make_async_copy(wgt_in, wgt, ls.at[1])
    fetch_wgt.start()
    total = jnp.zeros((B, 1), F32)
    for j in range(8):
        x = hid[:, j * W:(j + 1) * W].astype(F32)
        total = total + jnp.sum(x * x, axis=1, keepdims=True)
    rinv = lax.rsqrt(total * (1.0 / D) + EPS)
    rinv_t = jnp.transpose(jnp.broadcast_to(rinv, (B, B)))
    META[dp] = jnp.concatenate(
        [rinv_t[0:1, :], msk[...].astype(F32), tgt[...].astype(F32), jnp.zeros((5, B), F32)], axis=0)
    H[dp] = hid[:, pl.ds(pl.multiple_of(dp * W, W), W)]
    pl.semaphore_wait(barrier, 17)

    half = pl.ds(pl.multiple_of(co * 64, 64), 64)
    ohalf = pl.ds(pl.multiple_of((1 - co) * 64, 64), 64)
    hsend = []
    msend = []
    for k in range(1, 8):
        j = dp_peers[k - 1]
        c = rcopy(META.at[dp], META.at[dp], M0 + k, (j, seq))
        c.start()
        msend.append(c)
        c = rcopy(hid.at[half, pl.ds(pl.multiple_of(j * W, W), W)], H.at[dp, half, :], H0 + k, (j, seq))
        c.start()
        hsend.append(c)

    fetch_wgt.wait()
    for i in range(6):
        WP[i * G:(i + 1) * G, :] = wgt[i * G:(i + 1) * G, :]
    WP[6 * G:V - 8, :] = wgt[6 * G:V - 8, :]
    WP[V - 8:V + 8, :] = jnp.concatenate(
        [wgt[V - 8:V, :].astype(F32), jnp.zeros((8, W), F32)], axis=0).astype(BF16)
    WP[V + 8:VP, :] = jnp.zeros((VP - V - 8, W), BF16)
    gain_row = jnp.concatenate([gain[pl.ds(dp * 4 + i, 1), :] for i in range(4)], axis=1)
    GCOL[...] = jnp.transpose(jnp.broadcast_to(gain_row, (B, W)))
    STAT[...] = jnp.concatenate([jnp.full((1, CAP), LOW, F32), jnp.zeros((7, CAP), F32)], axis=0)
    DN[...] = jnp.zeros_like(DN)

    for k in range(1, 8):
        j = dp_from[k - 1]
        rcopy(META.at[j], META.at[j], M0 + k, (dp, seq)).wait_recv()
    metas = [META[j] for j in range(8)]
    m8 = jnp.concatenate([m[1:2, :] for m in metas] + [jnp.zeros((8, B), F32)], axis=0)
    tri = (lax.broadcasted_iota(jnp.int32, (B, B), 0) <= lax.broadcasted_iota(jnp.int32, (B, B), 1)).astype(F32)
    cum = jnp.dot(m8.astype(BF16), tri.astype(BF16), preferred_element_type=F32)
    base = jnp.zeros((1, 1), F32)
    slot = lax.broadcasted_iota(jnp.int32, (CAP, B), 0)
    for j in range(8):
        rank = jnp.where(metas[j][1:2, :] > 0.5, cum[j:j + 1, :] + base - 1.0, -1.0).astype(jnp.int32)
        S[:, j * B:(j + 1) * B] = (slot == rank).astype(F32).astype(BF16)
        base = base + jnp.sum(metas[j][1:2, :], axis=1, keepdims=True)
    count = base
    r_all = jnp.concatenate([m[0:1, :] for m in metas], axis=1)
    v_all = jnp.concatenate([m[1:2, :] for m in metas], axis=1)
    t_all = jnp.concatenate([m[2:3, :] for m in metas], axis=1)
    hi = r_all.astype(BF16).astype(F32)
    mid = (r_all - hi).astype(BF16).astype(F32)
    lo = (r_all - hi) - mid
    ta = jnp.floor(t_all * (1.0 / 4096))
    tb = jnp.floor((t_all - ta * 4096) * (1.0 / 64))
    tc = t_all - ta * 4096 - tb * 64
    mr = jnp.concatenate([hi, mid, lo, v_all, ta, tb, tc, jnp.zeros((9, 8 * B), F32)], axis=0).astype(BF16)
    crow = lax.dot_general(mr, S[...], NT, preferred_element_type=F32)
    mr2 = jnp.concatenate([mr, jnp.zeros((B - 16, 8 * B), BF16)], axis=0)
    ccol = lax.dot_general(S[...], mr2, NT, preferred_element_type=F32)
    valid_row = crow[3:4, :]
    tgt_f = crow[4:5, :] * 4096.0 + crow[5:6, :] * 64.0 + crow[6:7, :] - (seq * V).astype(F32)
    here = jnp.logical_and(valid_row > 0.5, jnp.logical_and(tgt_f > -0.5, tgt_f < V - 0.5))
    tgt_f = jnp.where(here, tgt_f, -1.0)
    rinv_col = ccol[:, 0:1] + ccol[:, 1:2] + ccol[:, 2:3]
    ROWS[...] = jnp.concatenate(
        [crow[0:1, :] + crow[1:2, :] + crow[2:3, :], valid_row / count, tgt_f, valid_row,
         jnp.zeros((4, CAP), F32)], axis=0)

    hc = []
    for k in range(1, 8):
        j = dp_from[k - 1]
        rcopy(H.at[j, half, :], H.at[j, half, :], H0 + k, (dp, seq)).wait_recv()
        c = rcopy(H.at[j, half, :], H.at[j, half, :], HC0 + k, core_dev)
        c.start()
        hc.append(c)
    for k in range(1, 8):
        j = dp_from[k - 1]
        rcopy(H.at[j, ohalf, :], H.at[j, ohalf, :], HC0 + k, core_dev).wait_recv()
    hcomp = jnp.dot(S[...], H[...].reshape(8 * B, W), preferred_element_type=F32)
    C[...] = ((hcomp * rinv_col) * gain_row).astype(BF16)

    def axis(c, s):
        a = (c + s) % 3
        e0, e1, e2 = (2 - a) * (1 - a) // 2, a * (2 - a), a * (a - 1) // 2
        return p1 * e0 + p2 * e1 + xh * e2, (ya * e0 + yb * e1 + xpeer * e2, seq)

    def bits(c):
        return axis(c, 0)[0], axis(c, 1)[0], axis(c, 2)[0]

    def s1(c):
        f, g, h = bits(c)
        return rcopy(L.at[rows_at(c * R + (1 - f) * RH, RH), :], R1.at[c], S10 + c, axis(c, 0)[1])

    def s2(c):
        f, g, h = bits(c)
        return rcopy(A1.at[c, rows_at((1 - g) * RQ, RQ), :], R2.at[c], S20 + c, axis(c, 1)[1])

    def s3(c):
        f, g, h = bits(c)
        return rcopy(A2.at[c, rows_at((1 - h) * RP, RP), :], R3.at[c], S30 + c, axis(c, 2)[1])

    def within(start, size, sem, dev):
        return rcopy(PR.at[rows_at(start, size), :], PR.at[rows_at(start, size), :], sem, dev)

    def g3(c, other=0):
        f, g, h = bits(c)
        h = h + other * (1 - 2 * h)
        return within(c * R + f * RH + g * RQ + h * RP, RP, G30 + c, axis(c, 2)[1])

    def g2(c, other=0):
        f, g, h = bits(c)
        g = g + other * (1 - 2 * g)
        return within(c * R + f * RH + g * RQ, RQ, G20 + c, axis(c, 1)[1])

    def g1(c, other=0):
        f, g, h = bits(c)
        f = f + other * (1 - 2 * f)
        return within(c * R + f * RH, RH, G10 + c, axis(c, 0)[1])

    def gather_steps(k):
        @pl.when(jnp.logical_and(k >= LAG4, k < CH + LAG4))
        def _():
            g3(k - LAG4, 1).wait_recv()
            g2(k - LAG4).start()

        @pl.when(jnp.logical_and(k >= LAG5, k < CH + LAG5))
        def _():
            g2(k - LAG5, 1).wait_recv()
            g1(k - LAG5).start()

    @pl.loop(0, CH + LAG3)
    def _(k):
        @pl.when(k < CH)
        def _():
            rows = rows_at(k * R, R)
            L[rows, :] = lax.dot_general(WP[rows, :], C[...], NT, preferred_element_type=F32).astype(BF16)
            s1(k).start()

        @pl.when(jnp.logical_and(k >= LAG1, k < CH + LAG1))
        def _():
            c = k - LAG1
            f, g, h = bits(c)
            s1(c).wait_recv()
            A1[c] = (L[rows_at(c * R + f * RH, RH), :].astype(F32) + R1[c].astype(F32)).astype(BF16)
            s2(c).start()

        @pl.when(jnp.logical_and(k >= LAG2, k < CH + LAG2))
        def _():
            c = k - LAG2
            f, g, h = bits(c)
            s2(c).wait_recv()
            A2[c] = (A1[c, rows_at(g * RQ, RQ), :].astype(F32) + R2[c].astype(F32)).astype(BF16)
            s3(c).start()

        @pl.when(k >= LAG3)
        def _():
            c = k - LAG3
            f, g, h = bits(c)
            s3(c).wait_recv()
            logits = A2[c, rows_at(h * RP, RP), :].astype(F32) + R3[c].astype(F32)
            first = c * R + f * RH + g * RQ + h * RP
            local = first + lax.broadcasted_iota(jnp.int32, (RP, CAP), 0)
            inside = local < V
            ex = jnp.where(inside, jnp.exp(logits), 0.0)
            PR[rows_at(first, RP), :] = ex.astype(BF16)
            g3(c).start()
            hit = local == ROWS[2:3, :].astype(jnp.int32)
            STAT[0:1, :] = jnp.maximum(
                STAT[0:1, :], jnp.max(jnp.where(inside, logits, LOW), axis=0, keepdims=True))
            STAT[1:2, :] = STAT[1:2, :] + jnp.sum(ex, axis=0, keepdims=True)
            STAT[2:3, :] = STAT[2:3, :] + jnp.sum(ex * logits, axis=0, keepdims=True)
            STAT[3:4, :] = STAT[3:4, :] + jnp.sum(jnp.where(hit, logits, 0.0), axis=0, keepdims=True)

        gather_steps(k)

    def merge(slots, n):
        parts = [slots[i] for i in range(n)]
        top = parts[0][0:1, :]
        sums = parts[0][1:4, :]
        for q in parts[1:]:
            top = jnp.maximum(top, q[0:1, :])
            sums = sums + q[1:4, :]
        return jnp.concatenate([top, sums, jnp.zeros((4, CAP), F32)], axis=0)

    sends = []

    def spread(slots, mine, devs, sem):
        for k, dev in enumerate(devs, 1):
            c = rcopy(slots.at[mine], slots.at[mine], sem + k, dev)
            c.start()
            sends.append(c)

    def collect(slots, froms, sem):
        for k, src in enumerate(froms, 1):
            rcopy(slots.at[src], slots.at[src], sem + k, (dp, seq)).wait_recv()

    last = CH + LAG3
    mids = [last + (LAG5 - LAG3) * i // 3 for i in range(4)]
    ST1[g_me] = STAT[...]
    spread(ST1, g_me, [(dp, z * 4 + g) for g in g_peers], T10)
    HCT[...] = jnp.transpose(hcomp)

    @pl.loop(mids[0], mids[1])
    def _(k):
        gather_steps(k)
    collect(ST1, g_from, T10)
    ST2[z] = merge(ST1, 4)
    spread(ST2, z, [(dp, seq_of(zz, xl, co)) for zz in z_peers], T20)

    @pl.loop(0, VP // G)
    def _(i):
        WT[i] = jnp.transpose(WP[pl.ds(pl.multiple_of(i * G, G), G), :])

    @pl.loop(mids[1], mids[2])
    def _(k):
        gather_steps(k)
    collect(ST2, z_from, T20)
    ST3[dp] = merge(ST2, 8)
    spread(ST3, dp, [(j, seq) for j in dp_peers], T30)

    @pl.loop(mids[2], mids[3])
    def _(k):
        gather_steps(k)
    collect(ST3, dp_from, T30)
    stat = merge(ST3, 8)
    top, ssum, esum, tsum = [stat[i:i + 1, :] for i in range(4)]
    share = ROWS[1:2, :]
    valid = ROWS[3:4, :] > 0.5
    loss = jnp.sum(jnp.where(valid, jnp.log(ssum) - tsum, 0.0), axis=1, keepdims=True) / count
    size = jnp.abs(top)
    peak = (1.0 + size) * jnp.exp(top) / ssum
    odd = jnp.where(jnp.logical_and(valid, jnp.logical_or(size > 40.0, peak > 0.25)), 1.0, 0.0)
    odd = jnp.maximum(jnp.max(odd, axis=1, keepdims=True), jnp.where(count > CAP + 0.5, 1.0, 0.0))
    scal[...] = loss
    flag[...] = odd.astype(jnp.int32)
    ROWS[4:5, :] = share / ssum
    ROWS[5:6, :] = (esum / ssum - tsum) * share * (1.0 / D)

    @pl.loop(0, VP // G)
    def _(i):
        for q in range(CH * G // VP):
            g1(i * (CH * G // VP) + q, 1).wait_recv()
        rows = rows_at(i * G, G)
        local = i * G + lax.broadcasted_iota(jnp.int32, (G, CAP), 0)
        hit = local == ROWS[2:3, :].astype(jnp.int32)
        dl = PR[rows, :].astype(F32) * ROWS[4:5, :] - jnp.where(hit, ROWS[1:2, :], 0.0)
        dlo[rows, :] = dl.astype(BF16)
        DN[...] += jnp.dot(WT[i], dlo[rows, :], preferred_element_type=F32)

    pass_on, keep = (1 - xl) * 128, xl * 128
    dc = []
    for n, start in enumerate((pass_on, keep)):
        c = rcopy(DN.at[rows_at((1 - co) * 256 + start, 128), :], RC.at[rows_at(start, 128), :], DC0 + n, core_dev)
        c.start()
        dc.append(c)
    dc[0].wait_recv()
    far = (4, 3, 5, 2, 6, 1, 7, 0)
    dx = []
    for n, k in enumerate(far):
        zz = lax.rem(z + k, 8)
        at = pass_on + zz * 16
        B1[zz] = DN[rows_at(co * 256 + at, 16), :] + RC[rows_at(at, 16), :]
        c = rcopy(B1.at[zz], RX.at[zz], DX0 + n, xlo_dev)
        c.start()
        dx.append(c)
    dc[1].wait_recv()
    T1[...] = DN[rows_at(co * 256 + keep, 128), :] + RC[rows_at(keep, 128), :]
    dz = []
    for n, k in enumerate(far):
        zz = lax.rem(z + k, 8)
        dx[n].wait_recv()
        part = T1[rows_at(zz * 16, 16), :] + RX[zz]
        if k:
            B2[zz] = part
            c = rcopy(B2.at[zz], RZ.at[z], DZ0 + k, (dp, seq_of(zz, xl, co)))
            c.start()
            dz.append(c)
    dn = part
    for k in (1, 7, 2, 6, 3, 5, 4):
        rcopy(RZ.at[z_from[k - 1]], RZ.at[z_from[k - 1]], DZ0 + k, (dp, seq)).wait_recv()
        dn = dn + RZ[z_from[k - 1]]

    off = co * 256 + xl * 128 + z * 16
    rinv_row = ROWS[0:1, :]
    xn = HCT[rows_at(off, 16), :] * rinv_row
    gc = GCOL[rows_at(off, 16), 0:1]
    grow = (rinv_row * (dn * gc - xn * ROWS[5:6, :])).astype(BF16)
    ggc = jnp.sum(dn * xn, axis=1, keepdims=True)
    wide_rows = jnp.dot(grow, S[...], preferred_element_type=F32).astype(BF16)
    ghi = ggc.astype(BF16).astype(F32)
    gmid = (ggc - ghi).astype(BF16).astype(F32)
    glo = (ggc - ghi) - gmid
    lane = lax.broadcasted_iota(jnp.int32, (16, B), 1)
    gparts = jnp.where(lane == 0, ghi, jnp.where(lane == 1, gmid, jnp.where(lane == 2, glo, 0.0))).astype(BF16)
    for j in range(8):
        MB[j, 0:16, :] = wide_rows[:, j * B:(j + 1) * B]
        MB[j, 16:32, :] = gparts
    dpc = []
    for k in range(1, 8):
        c = rcopy(MB.at[dp_peers[k - 1]], RB.at[dp], DP0 + k, (dp_peers[k - 1], seq))
        c.start()
        dpc.append(c)
    RB[dp] = MB[dp]
    for k in range(1, 8):
        rcopy(RB.at[dp_from[k - 1]], RB.at[dp_from[k - 1]], DP0 + k, (dp, seq)).wait_recv()

    mine = co * 16 + xl * 8 + z
    GTX[mine, 0:B, :] = RB[:, 0:16, :].reshape(B, B)
    GTX[mine, B:B + 16, :] = jnp.transpose(RB[:, 16:32, :].reshape(B, B).astype(F32))[0:16, :].astype(BF16)

    def slice_copy(i, sem, dev):
        return rcopy(GTX.at[i], GTX.at[i], sem, dev)

    def forward(i, sem, dev):
        c = slice_copy(i, sem, dev)
        c.start()
        sends.append(c)

    row = lax.broadcasted_iota(jnp.int32, (B, B), 0)
    lane = lax.broadcasted_iota(jnp.int32, (B, B), 1)
    pick = (row == lane // 16).astype(F32)
    diag = row % 16 == lane % 16

    def emit(cc, xx):
        q = cc * 2 + xx
        at = pl.ds(q * 8, 8)
        for j in range(8):
            block = GTX[at, j * 16:(j + 1) * 16, :].reshape(B, B)
            ghid[:, pl.ds(pl.multiple_of(j * W + q * B, B), B)] = jnp.transpose(block)
        parts = GTX[at, B:B + 16, :].astype(F32)
        sums = parts[:, 0, :] + parts[:, 1, :] + parts[:, 2, :]
        cols = jnp.transpose(jnp.concatenate([sums, jnp.zeros((B - 8, B), F32)], axis=0))
        spread = jnp.dot(cols, pick, precision=lax.Precision.HIGHEST, preferred_element_type=F32)
        spread = jnp.sum(jnp.where(diag, spread, 0.0).reshape(8, 16, B), axis=1)
        for j in range(8):
            gg[pl.ds(j * 4 + q, 1), :] = spread[j:j + 1, :]

    near = (1, 7, 2, 6, 3, 5, 4)
    ox, oc = 1 - xl, 1 - co
    for k in (4, 3, 5, 2, 6, 1, 7):
        forward(mine, AZ0 + k, (dp, seq_of(z_peers[k - 1], xl, co)))
    forward(mine, AX0, xlo_dev)
    forward(mine, AC0, core_dev)
    for k in near:
        src = co * 16 + xl * 8 + z_from[k - 1]
        slice_copy(src, AZ0 + k, (dp, seq)).wait_recv()
        forward(src, AX0 + k, xlo_dev)
        forward(src, AC0 + k, core_dev)
    emit(co, xl)
    for k in (0,) + near:
        src = co * 16 + ox * 8 + (z_from[k - 1] if k else z)
        slice_copy(src, AX0 + k, (dp, seq)).wait_recv()
        forward(src, AC0 + 8 + k, core_dev)
    emit(co, ox)
    for k in (0,) + near:
        slice_copy(oc * 16 + xl * 8 + (z_from[k - 1] if k else z), AC0 + k, (dp, seq)).wait_recv()
    emit(oc, xl)
    for k in (0,) + near:
        slice_copy(oc * 16 + ox * 8 + (z_from[k - 1] if k else z), AC0 + 8 + k, (dp, seq)).wait_recv()
    emit(oc, ox)

    for c in hsend + msend + hc + sends + dc + dx + dz + dpc:
        c.wait_send()

    @pl.loop(0, CH)
    def _(c):
        s1(c).wait_send()
        s2(c).wait_send()
        s3(c).wait_send()
        g3(c).wait_send()
        g2(c).wait_send()
        g1(c).wait_send()


def fused(hidden, gain, head_weight, targets, loss_mask):
    vm = pl.BlockSpec(memory_space=pltpu.VMEM)
    hbm = pl.BlockSpec(memory_space=pl.ANY)
    scratch = [
        pltpu.VMEM((B, D), BF16),
        pltpu.VMEM((V, W), BF16),
        pltpu.VMEM((32, B + 16, B), BF16),
        pltpu.VMEM((8, B, W), BF16),
        pltpu.VMEM((8, 8, B), F32),
        pltpu.VMEM((VP, W), BF16),
        pltpu.VMEM((VP // G, W, G), BF16),
        pltpu.VMEM((CAP, 8 * B), BF16),
        pltpu.VMEM((W, CAP), F32),
        pltpu.VMEM((W, B), F32),
        pltpu.VMEM((8, CAP), F32),
        pltpu.VMEM((VP, CAP), BF16),
        pltpu.VMEM((CH, RH, CAP), BF16),
        pltpu.VMEM((CH, RH, CAP), BF16),
        pltpu.VMEM((CH, RQ, CAP), BF16),
        pltpu.VMEM((CH, RQ, CAP), BF16),
        pltpu.VMEM((CH, RP, CAP), BF16),
        pltpu.VMEM((8, CAP), F32),
        pltpu.VMEM((4, 8, CAP), F32),
        pltpu.VMEM((8, 8, CAP), F32),
        pltpu.VMEM((8, 8, CAP), F32),
        pltpu.VMEM((VP, CAP), BF16),
        pltpu.VMEM((W, CAP), F32),
        pltpu.VMEM((256, CAP), F32),
        pltpu.VMEM((128, CAP), F32),
        pltpu.VMEM((8, 16, CAP), F32),
        pltpu.VMEM((8, 16, CAP), F32),
        pltpu.VMEM((8, 16, CAP), F32),
        pltpu.VMEM((8, 16, CAP), F32),
        pltpu.VMEM((8, 32, B), BF16),
        pltpu.VMEM((8, 32, B), BF16),
        pltpu.SemaphoreType.DMA((NSEM,)),
        pltpu.SemaphoreType.DMA((NSEM,)),
        pltpu.SemaphoreType.DMA((2,)),
    ]
    return pl.pallas_call(
        kernel,
        out_shape=(
            jax.ShapeDtypeStruct((VP, CAP), BF16),
            jax.ShapeDtypeStruct((CAP, W), BF16),
            jax.ShapeDtypeStruct((B, D), BF16),
            jax.ShapeDtypeStruct((32, B), F32),
            jax.ShapeDtypeStruct((1, 1), F32),
            jax.ShapeDtypeStruct((1, 1), jnp.int32),
        ),
        in_specs=[hbm, vm, hbm, vm, vm],
        out_specs=(vm,) * 6,
        scratch_shapes=scratch,
        compiler_params=pltpu.CompilerParams(
            collective_id=0, has_side_effects=True, vmem_limit_bytes=44 * 1024 * 1024),
        cost_estimate=pl.CostEstimate(flops=6 * V * CAP * W, bytes_accessed=16 * 1024 * 1024, transcendentals=0),
        name="fused",
    )(hidden, gain.reshape(32, B), head_weight, targets.reshape(1, B), loss_mask.reshape(1, B))


STEPS = 4


def finish_kernel(dl, c, ghid, gg, scal, gh, ghid_out, gg_out, loss, fs):
    i = pl.program_id(0)
    n = VP // STEPS
    rows = pltpu.make_async_copy(ghid, ghid_out, fs.at[0])

    @pl.when(i == 0)
    def _():
        rows.start()
        gg_out[...] = gg[...]
        loss[...] = scal[...]

    gh[...] = jnp.dot(dl[pl.ds(pl.multiple_of(i * n, 16), n), :], c[...], preferred_element_type=F32)

    @pl.when(i == STEPS - 1)
    def _():
        rows.wait()


def finish(dl, c, ghid, gg, scal):
    vm = pl.BlockSpec(memory_space=pltpu.VMEM)
    n = VP // STEPS
    return pl.pallas_call(
        finish_kernel,
        grid=(STEPS,),
        out_shape=(
            jax.ShapeDtypeStruct((V, W), F32),
            jax.ShapeDtypeStruct((B, D), BF16),
            jax.ShapeDtypeStruct((32, B), F32),
            jax.ShapeDtypeStruct((1, 1), F32),
        ),
        in_specs=[vm] * 5,
        out_specs=(
            pl.BlockSpec((n, W), lambda i: (i, 0)),
            pl.BlockSpec(memory_space=pltpu.HBM),
            pl.BlockSpec((32, B), lambda i: (0, 0)),
            pl.BlockSpec((1, 1), lambda i: (0, 0)),
        ),
        scratch_shapes=[pltpu.SemaphoreType.DMA((1,))],
        compiler_params=pltpu.CompilerParams(vmem_limit_bytes=40 * 1024 * 1024),
        cost_estimate=pl.CostEstimate(flops=2 * V * CAP * W, bytes_accessed=8 * 1024 * 1024, transcendentals=0),
        name="finish",
    )(dl, c, ghid, gg, scal)


def norm_back(grad_normed, unit_rows, inv_rms, gain):
    grad_unit = grad_normed * gain
    return inv_rms * (
        grad_unit - unit_rows * jnp.mean(grad_unit * unit_rows, axis=-1, keepdims=True)
    )


def spread_all(x, name):
    n = lax.axis_size(name)
    copies = jnp.broadcast_to(x[None], (n,) + x.shape)
    return lax.all_to_all(copies, name, split_axis=0, concat_axis=0, tiled=True)


def scatter_sum(x, name):
    n = lax.axis_size(name)
    parts = lax.all_to_all(x, name, split_axis=0, concat_axis=0, tiled=True)
    return jnp.sum(parts.reshape((n, x.shape[0] // n) + x.shape[1:]), axis=0)


def total(x, name):
    return jnp.sum(spread_all(x, name), axis=0)


def general(hidden, gain, head_weight, targets, loss_mask):
    floats = hidden.astype(jnp.float32)
    inv_rms = lax.rsqrt(jnp.mean(floats * floats, axis=-1, keepdims=True) + EPS)
    unit_rows = floats * inv_rms
    normed = (unit_rows * gain).astype(jnp.bfloat16)
    mask_float = loss_mask.astype(jnp.float32)
    num_valid = total(jnp.sum(mask_float).reshape(1), "dp")[0]
    slices = lax.all_to_all(normed, "dp", split_axis=1, concat_axis=0, tiled=True)
    vocab_rows = head_weight.shape[0]
    logits = scatter_sum(
        lax.dot_general(slices, head_weight, NT, preferred_element_type=jnp.float32), "dp")
    column = lax.axis_index("seq") * vocab_rows + jnp.arange(vocab_rows, dtype=jnp.int32)
    one_hot = (column[None, :] == targets[:, None]).astype(jnp.float32)
    local_picked = jnp.sum(one_hot * logits, axis=1)
    row_top = jnp.max(spread_all(jnp.max(logits, axis=1), "seq"), axis=0)
    shifted = jnp.exp(logits - row_top[:, None])
    row_total, picked = total(jnp.stack([jnp.sum(shifted, axis=1), local_picked]), "seq")
    log_total = row_top + jnp.log(row_total)
    probs = shifted / row_total[:, None]
    row_loss = log_total - picked
    loss_value = total(jnp.sum(mask_float * row_loss).reshape(1), "dp")[0] / num_valid
    dlogits = ((probs - one_hot) * (mask_float / num_valid)[:, None]).astype(jnp.bfloat16)
    shard_rows = spread_all(dlogits, "dp").reshape(-1, vocab_rows)
    grad_slices = jnp.dot(shard_rows, head_weight, preferred_element_type=jnp.float32)
    grad_head = lax.dot_general(
        shard_rows, slices, (((0,), (0,)), ((), ())), preferred_element_type=jnp.float32
    )
    returned = lax.all_to_all(grad_slices, "dp", split_axis=0, concat_axis=1, tiled=True)
    mine = scatter_sum(returned, "seq")
    grad_normed = spread_all(mine, "seq").reshape(returned.shape)
    grad_gain = total(jnp.sum(grad_normed * unit_rows, axis=0), "dp")
    grad_hidden = norm_back(grad_normed, unit_rows, inv_rms, gain).astype(jnp.bfloat16)
    return (loss_value, grad_hidden, grad_gain, grad_head)


def body(hidden, gain, head_weight, targets, loss_mask):
    dl, c, ghid, gg, scal, flag = fused(hidden, gain, head_weight, targets, loss_mask)

    def fast(*args):
        gh, ghid_out, gg_out, loss = finish(dl, c, ghid, gg, scal)
        return loss.reshape(()), ghid_out, gg_out.reshape(D), gh

    return lax.cond(flag[0, 0] > 0, general, fast, hidden, gain, head_weight, targets, loss_mask)


def solution(mesh):
    return jax.shard_map(
        body,
        mesh=mesh,
        in_specs=(P("dp", None), P(), P("seq", "dp"), P("dp"), P("dp")),
        out_specs=(P(), P("dp", None), P(), P("seq", "dp")),
        check_vma=False,
    )
```
